128 devices in a mesh: row: 16 (over y, z), col: 8 (over x, core).
Axes of the slice: x: 4, y: 4, z: 4, core: 2. Of those that a mesh axis runs over, the one named last changes fastest.
Arguments:
- atoms: bfloat16 [16384, 128], P(('row', 'col')), may hold values from -6 to 6
- atom_bias: bfloat16 [4, 16384, 128], P(None, ('row', 'col')), may hold values from -8 to 250
- key_shift: int32 [512], P(('row', 'col')), may hold values from -16 to 16, as said below
- atom_token: int32 [16384], P(('row', 'col')), may hold values from 0 to 2047, as said below
- token_atoms: int32 [2048], P(('row', 'col')), may hold values from 1 to 209, as said below
- token_mask: int32 [2048], P(('row', 'col')), may hold values from 0 to 1, as said below
- pair: bfloat16 [2048, 16, 8, 16, 128], P('row', None, 'col'), may hold values from -45 to 45
- w_atom_qkv: bfloat16 [128, 384], replicated, may hold values from -0.5 to 0.5
- w_atom_out: bfloat16 [128, 128], replicated, may hold values from -0.5 to 0.5
- w_pool: bfloat16 [128, 768], replicated, may hold values from -0.5 to 0.5
- w_token_qkv: bfloat16 [768, 2304], replicated, may hold values from -0.21875 to 0.21875
- w_token_out: bfloat16 [768, 768], replicated, may hold values from -0.21875 to 0.21875
- w_bias: bfloat16 [128, 16], replicated, may hold values from -1 to 1
- w_back: bfloat16 [768, 128], replicated, may hold values from -0.21875 to 0.21875
- cotangent: bfloat16 [16384, 128], P(('row', 'col')), may hold values from -768 to 768
Outputs:
- atom_out: bfloat16 [16384, 128], P(('row', 'col'))
- pair_grad: bfloat16 [2048, 16, 8, 16, 128], P('row', None, 'col')
The draws below stay inside these ranges and needn't reach their ends.
Inputs may be any that keep to these rules, and one draw needn't show every extreme that they name: `atom_token`: never falling. The atoms of the 16 tokens 16 * e to 16 * e + 15 form one run that begins within 48 atoms of atom 8 * 16 * e and ends within 48 atoms of atom 8 * 16 * (e + 1); every token has at least one atom. In every draw the tokens of the second device run into the atoms of both of its neighbours. `token_atoms`: the number of atoms a with atom_token[a] equal to the token; the most is taken in every draw. `key_shift`: both ends of the range are taken in every draw. `token_mask`: between 128 and 512 tokens are 0, anywhere among the tokens.
All inputs are finite; a program needn't handle non-finite values.
Results may differ from the reference program's by a relative error of at most 0.0187.
Values may be sent and summed in bfloat16 or wider, within the bound.
No kernel may reach another device: no remote copies, remote signals or barrier semaphores. Data moves between devices by JAX's collectives and lax.ppermute only.
A program may use at most 128 MiB of HBM per device.

```python
import math
import jax
import jax.numpy as jnp
from jax import lax

CA = 128
HA = 4
DA = 32
CT = 768
HT = 16
DT = 48
CZ = 128
QB = 32
KW = 128
SHIFT = 16
TOK_DEV = 16
ATOM_DEV = 128
NTOK = 2048
NATOM = 16384
ROWT = 128
COLT = 256


def atom_layout(key):
    devices = NTOK // TOK_DEV
    largest = 3 * TOK_DEV
    offsets = jax.random.randint(jax.random.fold_in(key, 11), (devices + 1,), -largest, largest + 1)
    offsets = offsets.at[0].set(0).at[devices].set(0).at[1].set(-largest).at[2].set(largest)
    borders = jnp.arange(devices + 1, dtype=jnp.int32) * ATOM_DEV + offsets
    lengths = borders[1:] - borders[:-1]
    random_ints = jax.random.randint(jax.random.fold_in(key, 12), (devices, TOK_DEV - 1), 0, 1 << 20)
    chosen = jnp.sort(random_ints % (lengths[:, None] - TOK_DEV + 1), axis=1)
    chosen = chosen.at[1].set(lengths[1] - TOK_DEV)
    splits = chosen + jnp.arange(1, TOK_DEV, dtype=jnp.int32)[None, :]
    starts = jnp.concatenate([jnp.zeros((devices, 1), jnp.int32), splits], axis=1) + borders[:-1, None]
    starts = starts.reshape(NTOK).astype(jnp.int32)
    ends_at = jnp.concatenate([starts[1:], jnp.full((1,), NATOM, jnp.int32)])
    owners = jnp.searchsorted(starts, jnp.arange(NATOM, dtype=jnp.int32), side='right') - 1
    return (owners.astype(jnp.int32), (ends_at - starts).astype(jnp.int32))


def draw_atom_token(key, part):
    return atom_layout(key)[0]


def draw_token_atoms(key, part):
    return atom_layout(key)[1]


def draw_key_shift(key, part):
    key = jax.random.fold_in(key, 3)
    blocks = NATOM // QB
    shifts = jax.random.randint(key, (blocks,), -SHIFT, SHIFT + 1)
    residue = jnp.arange(blocks, dtype=jnp.int32) % 7
    shifts = jnp.where(residue == 3, SHIFT, jnp.where(residue == 5, -SHIFT, shifts))
    return shifts.astype(jnp.int32)


def draw_token_mask(key, part):
    key = jax.random.fold_in(key, 5)
    count_key, order_key = jax.random.split(key)
    padding = jax.random.randint(count_key, (), NTOK // 16, NTOK // 4 + 1)
    ranking = jax.random.permutation(order_key, NTOK).astype(jnp.int32)
    return (ranking >= padding).astype(jnp.int32)


def draw_atom_bias(key, part):
    key = jax.random.fold_in(key, 7)
    shape = (HA, NATOM, KW)
    values = jax.random.normal(key, shape, jnp.float32)
    return values.astype(jnp.bfloat16)


def draw_pair(key, part):
    key = jax.random.fold_in(key, 8)
    shape = (NTOK, NTOK, CZ)
    values = jax.random.normal(key, shape, jnp.float32)
    return values.reshape(NTOK, COLT // TOK_DEV, ROWT // TOK_DEV, TOK_DEV, CZ).astype(jnp.bfloat16)


def draw_w_bias(key, part):
    key = jax.random.fold_in(key, 9)
    spread = 1.0 / math.sqrt(CZ)
    values = jax.random.normal(key, (CZ, HT), jnp.float32) * spread
    return values.astype(jnp.bfloat16)


def shard_levels(stream_key, dims, shards, smallest, high):
    def one(dim, shards_of):
        heights = jax.random.uniform(jax.random.fold_in(jax.random.fold_in(stream_key, 6), dim), (shards_of,), jnp.float32, smallest / len(shards), high / len(shards))
        return jnp.repeat(jnp.exp(heights), dims[dim] // shards_of).reshape((-1,) + (1,) * (len(dims) - dim - 1))

    gain = one(*shards[0])
    for cut in shards[1:]:
        gain = gain * one(*cut)
    return gain


def noise(own_key, shape, deviation, bound, pieces=(), kind=jnp.bfloat16):
    values = deviation * jax.random.normal(own_key, shape, jnp.float32)
    if pieces:
        values = values * shard_levels(own_key, shape, pieces, -0.22, 0.18)
    return jnp.clip(values, -bound, bound).astype(kind)


def setup_inputs(seed: int = 0) -> dict:
    keys = jax.random.split(jax.random.key(seed), 16)
    atoms = noise(keys[0], (NATOM, CA), 1.0, 6.0, ((0, 128),))
    atom_bias = draw_atom_bias(jax.random.fold_in(keys[15], 71), 0)
    key_shift = draw_key_shift(jax.random.fold_in(keys[15], 71), 0)
    atom_token = draw_atom_token(jax.random.fold_in(keys[15], 71), 0)
    token_atoms = draw_token_atoms(jax.random.fold_in(keys[15], 71), 0)
    token_mask = draw_token_mask(jax.random.fold_in(keys[15], 71), 0)
    pair = draw_pair(jax.random.fold_in(keys[15], 71), 0)
    w_atom_qkv = noise(keys[7], (CA, 3 * CA), CA ** -0.5, 0.5)
    w_atom_out = noise(keys[8], (CA, CA), CA ** -0.5, 0.5)
    w_pool = noise(keys[9], (CA, CT), CA ** -0.5, 0.5)
    w_token_qkv = noise(keys[10], (CT, 3 * CT), CT ** -0.5, 0.21875)
    w_token_out = noise(keys[11], (CT, CT), CT ** -0.5, 0.21875)
    w_bias = draw_w_bias(jax.random.fold_in(keys[15], 71), 0)
    w_back = noise(keys[13], (CT, CA), CT ** -0.5, 0.21875)
    cotangent = noise(keys[14], (NATOM, CA), (NTOK // 16), 768.0, ((0, 128),))
    return {"atoms": atoms, "atom_bias": atom_bias, "key_shift": key_shift, "atom_token": atom_token, "token_atoms": token_atoms, "token_mask": token_mask, "pair": pair, "w_atom_qkv": w_atom_qkv, "w_atom_out": w_atom_out, "w_pool": w_pool, "w_token_qkv": w_token_qkv, "w_token_out": w_token_out, "w_bias": w_bias, "w_back": w_back, "cotangent": cotangent}


norm_epsilon = 1e-05

def layer_norm(values):
    values = values.astype(jnp.float32)
    centred = values - lax.optimization_barrier(jnp.mean(values, axis=-1, keepdims=True))
    return centred * lax.rsqrt(lax.optimization_barrier(jnp.mean(centred * centred, axis=-1, keepdims=True)) + norm_epsilon)

def softmax_rows(scores):
    row_max = lax.optimization_barrier(jnp.max(scores, axis=-1, keepdims=True))
    raised = jnp.exp(scores - row_max)
    return raised / lax.optimization_barrier(jnp.sum(raised, axis=-1, keepdims=True))

def atom_attention(atoms, atom_bias, key_shift, w_atom_qkv, w_atom_out):
    blocks = NATOM // QB
    normed = layer_norm(atoms).astype(jnp.bfloat16)
    project = jnp.dot(normed, w_atom_qkv, preferred_element_type=jnp.float32).astype(jnp.bfloat16)
    queries = project[:, :CA].reshape(blocks, QB, HA, DA)
    key_value = project[:, CA:]
    starts = jnp.arange(blocks, dtype=jnp.int32) * QB - (KW - QB) // 2 + key_shift
    positions = starts[:, None] + jnp.arange(KW, dtype=jnp.int32)[None, :]
    inside = (positions >= 0) & (positions < NATOM)
    windows = key_value[jnp.clip(positions, 0, NATOM - 1)]
    key_rows = windows[..., :CA].reshape(blocks, KW, HA, DA)
    value_rows = windows[..., CA:].reshape(blocks, KW, HA, DA)
    scores = jnp.einsum('bqhd,bkhd->hbqk', queries.astype(jnp.float32), key_rows.astype(jnp.float32)) / math.sqrt(DA)
    scores = scores + atom_bias.astype(jnp.float32).reshape(HA, blocks, QB, KW)
    scores = jnp.where(inside[None, :, None, :], scores, -jnp.inf)
    attend = softmax_rows(scores).astype(jnp.bfloat16)
    mixture = jnp.einsum('hbqk,bkhd->bqhd', attend.astype(jnp.float32), value_rows.astype(jnp.float32))
    mixture = mixture.reshape(NATOM, CA).astype(jnp.bfloat16)
    return (atoms.astype(jnp.float32) + jnp.dot(mixture, w_atom_out, preferred_element_type=jnp.float32)).astype(jnp.bfloat16)

def reference(atoms, atom_bias, key_shift, atom_token, token_atoms, token_mask, pair, w_atom_qkv, w_atom_out, w_pool, w_token_qkv, w_token_out, w_bias, w_back, cotangent):
    hidden = atom_attention(atoms, atom_bias, key_shift, w_atom_qkv, w_atom_out)
    lifted = jax.nn.relu(jnp.dot(hidden, w_pool, preferred_element_type=jnp.float32))
    pooled = jax.ops.segment_sum(lifted, atom_token, num_segments=NTOK) / token_atoms.astype(jnp.float32)[:, None]
    normed = layer_norm(pooled).astype(jnp.bfloat16)
    project = jnp.dot(normed, w_token_qkv, preferred_element_type=jnp.float32).astype(jnp.bfloat16)
    queries = project[:, :CT].reshape(NTOK, HT, DT).astype(jnp.float32)
    key_rows = project[:, CT:2 * CT].reshape(NTOK, HT, DT).astype(jnp.float32)
    value_rows = project[:, 2 * CT:].reshape(NTOK, HT, DT).astype(jnp.float32)
    live_keys = token_mask > 0
    grad_up = jax.ops.segment_sum(cotangent.astype(jnp.float32), atom_token, num_segments=NTOK).astype(jnp.bfloat16)
    grad_mid = jnp.dot(grad_up, w_back.T, preferred_element_type=jnp.float32).astype(jnp.bfloat16)
    grad_mix = jnp.dot(grad_mid, w_token_out.T, preferred_element_type=jnp.float32).astype(jnp.bfloat16)
    pair_flat = pair.reshape(NTOK, NTOK, CZ)
    bias_weight = w_bias.astype(jnp.float32)

    def one_block(row_start):
        pair_rows = lax.dynamic_slice_in_dim(pair_flat, row_start, ROWT, 0).astype(jnp.float32)
        pair_bias = jnp.einsum('ijc,ch->hij', pair_rows, bias_weight)
        block_queries = lax.dynamic_slice_in_dim(queries, row_start, ROWT, 0)
        scores = jnp.einsum('ihd,jhd->hij', block_queries, key_rows) / math.sqrt(DT) + pair_bias
        scores = jnp.where(live_keys[None, None, :], scores, -jnp.inf)
        row_max = lax.optimization_barrier(jnp.max(scores, axis=-1, keepdims=True))
        raised = jnp.exp(scores - row_max)
        totals = lax.optimization_barrier(jnp.sum(raised, axis=-1, keepdims=True))
        weighted = jnp.einsum('hij,jhd->ihd', raised.astype(jnp.bfloat16).astype(jnp.float32), value_rows)
        mixture = (weighted / jnp.transpose(totals[:, :, 0])[:, :, None]).reshape(ROWT, CT).astype(jnp.bfloat16)
        grad_heads = lax.dynamic_slice_in_dim(grad_mix, row_start, ROWT, 0).reshape(ROWT, HT, DT).astype(jnp.float32)
        grad_diag = jnp.einsum('ihd,ihd->hi', grad_heads, mixture.reshape(ROWT, HT, DT).astype(jnp.float32))
        grad_prob = jnp.einsum('ihd,jhd->hij', grad_heads, value_rows)
        grad_score = raised / totals * (grad_prob - grad_diag[:, :, None])
        block_grad = jnp.einsum('hij,ch->ijc', grad_score, bias_weight, precision=lax.Precision.HIGHEST)
        return (mixture, block_grad.astype(jnp.bfloat16))
    row_starts = jnp.arange(NTOK // ROWT, dtype=jnp.int32) * ROWT
    mixed_blocks, grad_blocks = lax.map(one_block, row_starts)
    token_mix = mixed_blocks.reshape(NTOK, CT)
    updated = (pooled + jnp.dot(token_mix, w_token_out, preferred_element_type=jnp.float32)).astype(jnp.bfloat16)
    lowered = jnp.dot(updated, w_back, preferred_element_type=jnp.float32)
    atom_out = (hidden.astype(jnp.float32) + lowered[atom_token]).astype(jnp.bfloat16)
    pair_grad = grad_blocks.reshape(pair.shape)
    return (atom_out, pair_grad)
```

```python
import functools
import math

import jax
import jax.numpy as jnp
from jax import lax
from jax.experimental import pallas as pl
from jax.experimental.pallas import tpu as pltpu
from jax.sharding import PartitionSpec as P

HA = 4
HT = 16
QB = 32
KW = 128
SHIFT = 16
HALF = 64
GROUP = 8
AUX = 16
EPSILON = 1e-05
LOWEST = -1e30
F32 = jnp.float32
BF16 = jnp.bfloat16
NT = (((1,), (1,)), ((), ()))
TN = (((0,), (0,)), ((), ()))

VMEM = pl.BlockSpec(memory_space=pltpu.VMEM)
SMEM = pl.BlockSpec(memory_space=pltpu.SMEM)


def params(mib):
    return pltpu.CompilerParams(vmem_limit_bytes=mib << 20)


def iota(shape, dim):
    return lax.broadcasted_iota(jnp.int32, shape, dim)


def dot(a, b, dims=None):
    if dims is None:
        return jnp.dot(a, b, preferred_element_type=F32)
    return lax.dot_general(a, b, dims, preferred_element_type=F32)


def normal(values):
    centred = values - jnp.mean(values, axis=-1, keepdims=True)
    return centred * lax.rsqrt(jnp.mean(centred * centred, axis=-1, keepdims=True) + EPSILON)


def split(values):
    high = values.astype(BF16)
    return high, (values - high.astype(F32)).astype(BF16)


def grouped_weight(head_rows, member):
    rows = iota(head_rows.shape, 0)
    return jnp.where(rows % GROUP == member, head_rows, 0.0).astype(BF16)


def pair_bias_kernel(pair_ref, head_ref, out_ref):
    head_rows = head_ref[...].astype(F32)
    weights = [
        jnp.concatenate(
            [grouped_weight(head_rows, 2 * p), grouped_weight(head_rows, 2 * p + 1)], axis=1
        )
        for p in range(GROUP // 2)
    ]
    for g in range(pair_ref.shape[0] // GROUP):
        total = None
        for p in range(GROUP // 2):
            row = g * GROUP + 2 * p
            both = jnp.concatenate([pair_ref[row], pair_ref[row + 1]], axis=1)
            part = dot(weights[p], both, NT)
            total = part if total is None else total + part
        out_ref[g] = total.reshape(HT, GROUP, total.shape[-1])


def pack_kernel(flag_ref, atoms_ref, bias_ref, cot_ref, aux_ref, near_ref, far_ref):
    def fill(out_ref, at):
        out_ref[0:128] = atoms_ref[...]
        for h in range(HA):
            out_ref[128 + HALF * h : 128 + HALF * (h + 1)] = bias_ref[h, at : at + HALF]
        out_ref[384:448] = cot_ref[at : at + HALF]
        out_ref[448:464] = aux_ref[...]

    @pl.when(flag_ref[0] == 1)
    def _():
        fill(near_ref, 0)
        fill(far_ref, HALF)

    @pl.when(flag_ref[0] == 0)
    def _():
        fill(near_ref, HALF)
        fill(far_ref, 0)


def atom_kernel(
    flag_ref,
    near_ref,
    far_ref,
    atoms_ref,
    bias_ref,
    cot_ref,
    aux_ref,
    count_ref,
    mask_ref,
    w_qkv_ref,
    w_out_ref,
    w_pool_ref,
    hidden_ref,
    pooled_ref,
    to_row_ref,
    to_col_ref,
    prev_ref,
    next_ref,
):
    @pl.when(flag_ref[0] == 1)
    def _():
        prev_ref[...] = near_ref[...]
        next_ref[...] = far_ref[...]

    @pl.when(flag_ref[0] == 0)
    def _():
        prev_ref[...] = far_ref[...]
        next_ref[...] = near_ref[...]

    first = flag_ref[1] * 128
    extended = jnp.concatenate([prev_ref[0:128], atoms_ref[...], next_ref[0:128]], axis=0)
    wide = extended.astype(F32)
    project = dot(normal(wide).astype(BF16), w_qkv_ref[...]).astype(BF16)
    head_lane = iota((QB, 128), 1) // 32
    head_mask = [jnp.where(head_lane == h, 1.0, 0.0) for h in range(HA)]
    slot = iota((1, KW), 1)
    offset = iota((KW, 160), 1) - iota((KW, 160), 0) - SHIFT
    mixes = []
    for block in (2, 3, 4, 5, 6, 7, 0, 1):
        if block < 2:
            source, local = prev_ref, block
            bias = [
                prev_ref[128 + HALF * h + 32 * local : 160 + HALF * h + 32 * local]
                for h in range(HA)
            ]
            shift = prev_ref[451 + local : 452 + local]
        elif block > 5:
            local = block - 6
            bias = [
                next_ref[128 + HALF * h + 32 * local : 160 + HALF * h + 32 * local]
                for h in range(HA)
            ]
            shift = next_ref[449 + local : 450 + local]
        else:
            local = block - 2
            bias = [bias_ref[h, 32 * local : 32 * local + 32] for h in range(HA)]
            shift = aux_ref[1 + local : 2 + local]
        shift = shift.astype(F32).astype(jnp.int32)
        pick = jnp.where(offset == shift[:, 0:1], 1.0, 0.0).astype(BF16)
        window = dot(pick, project[32 * block : 32 * block + 160, 128:]).astype(BF16)
        query = project[64 + 32 * block : 96 + 32 * block, :128].astype(F32)
        stacked = jnp.concatenate([query * head_mask[h] for h in range(HA)], axis=0).astype(BF16)
        scores = dot(stacked, window[:, :128], NT) * (1.0 / math.sqrt(32))
        scores = scores + jnp.concatenate(bias, axis=0).astype(F32)
        position = slot + (first + 32 * block - 112) + shift
        inside = (position >= 0) & (position < flag_ref[2])
        scores = jnp.where(inside, scores, LOWEST)
        raised = jnp.exp(scores - jnp.max(scores, axis=-1, keepdims=True))
        weight = (raised / jnp.sum(raised, axis=-1, keepdims=True)).astype(BF16)
        mixed = dot(weight, window[:, 128:])
        mix = mixed[0:32] * head_mask[0]
        for h in range(1, HA):
            mix = mix + mixed[32 * h : 32 * h + 32] * head_mask[h]
        mixes.append(mix)
    mixture = jnp.concatenate(mixes, axis=0).astype(BF16)
    base = jnp.concatenate([wide[128:320], wide[64:128]], axis=0)
    hidden = (base + dot(mixture, w_out_ref[...])).astype(BF16)
    hidden_ref[...] = hidden[:128]
    lifted = jnp.maximum(dot(hidden, w_pool_ref[...]), 0.0)
    own_token = aux_ref[0:1].astype(F32) - 17.0
    prev_token = prev_ref[448:449].astype(F32) - 33.0
    next_token = next_ref[448:449].astype(F32) - 1.0
    beside = jnp.where(iota((1, 128), 1) < HALF, next_token, prev_token)
    token = jnp.concatenate([own_token, beside], axis=1)
    select = jnp.where(iota((16, 256), 0).astype(F32) == token, 1.0, 0.0).astype(BF16)
    high, low = split(lifted)
    pooled = (dot(select, high) + dot(select, low)) / count_ref[...].astype(F32)
    pooled_ref[...] = pooled
    normed = normal(pooled).astype(BF16)
    cot = jnp.concatenate([cot_ref[...], next_ref[384:448], prev_ref[384:448]], axis=0)
    grad_up = dot(select, cot).astype(BF16)
    live = jnp.broadcast_to(mask_ref[...].astype(F32), (16, 128)).astype(BF16)
    for r in range(to_row_ref.shape[0]):
        to_row_ref[r, :, :768] = normed
        to_row_ref[r, :, 768:] = live
    for c in range(to_col_ref.shape[0]):
        to_col_ref[c, :, :768] = normed
        to_col_ref[c, :, 768:] = grad_up


def window_of(head):
    block, rest = divmod(head, 8)
    return 384 * block + (0 if rest < 5 else 128)


def token_kernel(
    keys_ref,
    rows_ref,
    bias_ref,
    w_qkv_ref,
    w_out_ref,
    w_back_ref,
    prob_ref,
    grad_ref,
    to_col_ref,
):
    normed = rows_ref[:, :768]
    query = dot(normed, w_qkv_ref[:, :768]).astype(BF16)
    key = dot(keys_ref[:, :768], w_qkv_ref[:, 768:1536]).astype(BF16)
    value = dot(keys_ref[:, :768], w_qkv_ref[:, 1536:]).astype(BF16)
    middle = dot(rows_ref[:, 768:], w_back_ref[...], NT).astype(BF16)
    grad = dot(middle, w_out_ref[...], NT).astype(BF16)
    live = keys_ref[:, 768:].astype(F32).T[0:1]
    closed = jnp.where(live > 0, 0.0, -jnp.inf)
    lane = iota((128, 256), 1)
    stat_lane = iota((128, 128), 1)
    mixed = [jnp.zeros((128, 128), F32) for _ in range(6)]
    tops = jnp.zeros((128, 128), F32)
    sums = jnp.zeros((128, 128), F32)
    diags = jnp.zeros((128, 128), F32)
    for h in range(HT):
        at = window_of(h)
        inside = (lane >= 48 * h - at) & (lane < 48 * (h + 1) - at)
        query_h = jnp.where(inside, query[:, at : at + 256].astype(F32), 0.0).astype(BF16)
        grad_h = jnp.where(inside, grad[:, at : at + 256].astype(F32), 0.0).astype(BF16)
        value_h = value[:, at : at + 256]
        scores = dot(query_h, key[:, at : at + 256], NT) * (1.0 / math.sqrt(48))
        scores = scores + bias_ref[:, h].reshape(128, 256) + closed
        top = jnp.maximum(jnp.max(scores, axis=-1, keepdims=True), LOWEST)
        high = top.astype(BF16).astype(F32)
        top = high + (top - high).astype(BF16).astype(F32)
        raised = jnp.exp(scores - top)
        grads = dot(grad_h, value_h, NT)
        prob_ref[:, h] = raised.reshape(16, GROUP, 256)
        grad_ref[:, h] = grads.reshape(16, GROUP, 256)
        total = jnp.sum(raised, axis=-1, keepdims=True)
        diag = jnp.sum(raised * grads, axis=-1, keepdims=True)
        out = jnp.where(inside, dot(raised.astype(BF16), value_h), 0.0)
        mixed[at // 128] = mixed[at // 128] + out[:, :128]
        mixed[at // 128 + 1] = mixed[at // 128 + 1] + out[:, 128:]
        here = stat_lane == h
        tops = jnp.where(here, top, tops)
        sums = jnp.where(here, total, sums)
        diags = jnp.where(here, diag, diags)
    stats = jnp.zeros((128, 128), F32)
    for k, part in enumerate((tops, sums, diags)):
        high = part.astype(BF16).astype(F32)
        for n, piece in enumerate((high, part - high)):
            turn = 32 * k + 16 * n
            stats = stats + (pltpu.roll(piece, turn, axis=1) if turn else piece)
    stats = stats.astype(BF16)
    blocks = [part.astype(BF16) for part in mixed]
    for c in range(8):
        for k in range(6):
            to_col_ref[c, :, 128 * k : 128 * (k + 1)] = blocks[k][16 * c : 16 * c + 16]
        for k in range(8):
            to_col_ref[c, :, 768 + 128 * k : 896 + 128 * k] = stats[16 * k : 16 * k + 16]


def merge_kernel(
    flag_ref, parts_ref, pooled_ref, w_out_ref, w_back_ref, scale_ref, diag_ref, low_ref, ratio_ref
):
    lane = iota((128, 128), 1)
    tops, sums, diags = [], [], []
    for c in range(8):
        part = jnp.concatenate(
            [parts_ref[c, :, 768 + 128 * k : 896 + 128 * k] for k in range(8)], axis=0
        ).astype(F32)
        part = part + pltpu.roll(part, 112, axis=1)
        tops.append(part)
        sums.append(pltpu.roll(part, 96, axis=1))
        diags.append(pltpu.roll(part, 64, axis=1))
    top = functools.reduce(jnp.maximum, tops)
    ratios = [jnp.where(lane < HT, jnp.exp(part - top), 0.0) for part in tops]
    total = functools.reduce(jnp.add, [r * s for r, s in zip(ratios, sums)])
    diag = functools.reduce(jnp.add, [r * d for r, d in zip(ratios, diags)])
    total = jnp.where(lane < HT, total, 1.0)
    inverse = 1.0 / total
    for c in range(8):
        ratio_ref[c] = ratios[c] * inverse
    col = flag_ref[0]
    scale_ref[...] = ratio_ref[col]
    diag_ref[...] = diag * inverse
    own = pl.ds(pl.multiple_of(col * 16, 16), 16)
    spread = jnp.where(iota((128, 768), 1) // 48 == iota((128, 768), 0), 1.0, 0.0).astype(BF16)
    high, low = split(jnp.concatenate([ratio_ref[c, own] for c in range(8)], axis=0))
    factor = dot(high, spread) + dot(low, spread)
    mixed = None
    for c in range(8):
        part = parts_ref[c, :, :768].astype(F32) * factor[16 * c : 16 * c + 16]
        mixed = part if mixed is None else mixed + part
    updated = (pooled_ref[...] + dot(mixed.astype(BF16), w_out_ref[...])).astype(BF16)
    high, low = split(dot(updated, w_back_ref[...]))
    low_ref[0] = high
    low_ref[1] = low


def pair_grad_kernel(prob_ref, grad_ref, scale_ref, diag_ref, head_ref, out_ref):
    head_rows = head_ref[...].astype(F32)
    weights = jnp.concatenate([grouped_weight(head_rows, i) for i in range(GROUP)], axis=1)
    for g in range(prob_ref.shape[0]):
        scale = scale_ref[g * GROUP : (g + 1) * GROUP]
        diag = diag_ref[g * GROUP : (g + 1) * GROUP]
        rows = []
        for h in range(HT):
            rows.append(
                prob_ref[g, h] * scale[:, h : h + 1] * (grad_ref[g, h] - diag[:, h : h + 1])
            )
        score = jnp.concatenate(rows, axis=0)
        result = dot(score.T.astype(BF16), weights)
        for i in range(GROUP):
            out_ref[g * GROUP + i] = result[:, 128 * i : 128 * (i + 1)].astype(BF16)


def atom_out_kernel(flag_ref, near_ref, far_ref, low_ref, aux_ref, hidden_ref, out_ref):
    odd = flag_ref[0] == 1
    near = near_ref[...].astype(F32)
    far = far_ref[...].astype(F32)
    before = jnp.where(odd, near, far).astype(BF16)
    after = jnp.where(odd, far, near).astype(BF16)
    rows = jnp.concatenate([before, low_ref[0], after, low_ref[1]], axis=0)
    token = aux_ref[0:1].astype(F32) - 1.0
    index = iota((64, 128), 0)
    index = jnp.where(index < 48, index, index - 32).astype(F32)
    select = jnp.where(index == token, 1.0, 0.0).astype(BF16)
    out_ref[...] = (hidden_ref[...].astype(F32) + dot(select, rows, TN)).astype(BF16)


def shards(
    atoms,
    atom_bias,
    key_shift,
    atom_token,
    token_atoms,
    token_mask,
    pair,
    w_atom_qkv,
    w_atom_out,
    w_pool,
    w_token_qkv,
    w_token_out,
    w_bias,
    w_back,
    cotangent,
):
    row_count, col_count = lax.axis_size("row"), lax.axis_size("col")
    devices = row_count * col_count
    device = lax.axis_index(("row", "col"))
    col = lax.axis_index("col")
    core_pairs = [(i, i ^ 1) for i in range(col_count)]
    chip_pairs = [(i, i + 1) for i in range(1, devices - 1, 2)]
    chip_pairs = chip_pairs + [(j, i) for i, j in chip_pairs]

    relative = (atom_token - 16 * device + 17).astype(BF16)
    aux = jnp.concatenate(
        [
            relative[None, :],
            jnp.broadcast_to(key_shift.astype(BF16)[:, None], (4, 128)),
            jnp.zeros((AUX - 5, 128), BF16),
        ],
        axis=0,
    )
    flags = jnp.stack([device % 2, device, jnp.int32(128) * devices]).astype(jnp.int32)
    payload = jax.ShapeDtypeStruct((464, 128), BF16)
    near, far = pl.pallas_call(
        pack_kernel,
        in_specs=[SMEM, VMEM, VMEM, VMEM, VMEM],
        out_specs=[VMEM, VMEM],
        out_shape=[payload, payload],
        name="pack",
        cost_estimate=pl.CostEstimate(flops=0, bytes_accessed=1 << 20, transcendentals=0),
    )(flags, atoms, atom_bias, cotangent, aux)
    near = lax.ppermute(near, "col", core_pairs)
    far = lax.ppermute(far, ("row", "col"), chip_pairs)

    tile = pair.reshape(128, 256, 128)
    head_rows = jnp.repeat(jnp.transpose(w_bias), GROUP, axis=0)
    steps = 8
    bias = pl.pallas_call(
        pair_bias_kernel,
        grid=(steps,),
        in_specs=[
            pl.BlockSpec((128 // steps, 256, 128), lambda i: (i, 0, 0)),
            pl.BlockSpec((128, 128), lambda i: (0, 0)),
        ],
        out_specs=pl.BlockSpec((16 // steps, HT, GROUP, 256), lambda i: (i, 0, 0, 0)),
        out_shape=jax.ShapeDtypeStruct((16, HT, GROUP, 256), F32),
        compiler_params=params(24),
        name="pair_bias",
        cost_estimate=pl.CostEstimate(
            flops=2 * 128 * 256 * 128 * 16 * 8, bytes_accessed=12 << 20, transcendentals=0
        ),
    )(tile, head_rows)

    hidden, pooled, to_row, to_col = pl.pallas_call(
        atom_kernel,
        in_specs=[SMEM] + [VMEM] * 11,
        out_specs=[VMEM] * 4,
        out_shape=[
            jax.ShapeDtypeStruct((128, 128), BF16),
            jax.ShapeDtypeStruct((16, 768), F32),
            jax.ShapeDtypeStruct((row_count, 16, 896), BF16),
            jax.ShapeDtypeStruct((col_count, 16, 896), BF16),
        ],
        scratch_shapes=[pltpu.VMEM((464, 128), BF16), pltpu.VMEM((464, 128), BF16)],
        compiler_params=params(24),
        name="atom_stage",
        cost_estimate=pl.CostEstimate(flops=1 << 28, bytes_accessed=2 << 20, transcendentals=1 << 17),
    )(
        flags,
        near,
        far,
        atoms,
        atom_bias,
        cotangent,
        aux,
        token_atoms[:, None],
        token_mask[:, None],
        w_atom_qkv,
        w_atom_out,
        w_pool,
    )
    rows = lax.all_to_all(to_col, "col", 0, 0).reshape(128, 896)
    keys = lax.all_to_all(to_row, "row", 0, 0).reshape(256, 896)

    table = jax.ShapeDtypeStruct((16, HT, GROUP, 256), F32)
    prob, grad, to_col = pl.pallas_call(
        token_kernel,
        in_specs=[VMEM] * 6,
        out_specs=[VMEM] * 3,
        out_shape=[table, table, jax.ShapeDtypeStruct((col_count, 16, 1792), BF16)],
        compiler_params=params(40),
        name="token_stage",
        cost_estimate=pl.CostEstimate(flops=1 << 31, bytes_accessed=12 << 20, transcendentals=1 << 19),
    )(keys, rows, bias, w_token_qkv, w_token_out, w_back)
    parts = lax.all_to_all(to_col, "col", 0, 0)

    stat = jax.ShapeDtypeStruct((128, 128), F32)
    scale, diag, low = pl.pallas_call(
        merge_kernel,
        in_specs=[SMEM] + [VMEM] * 4,
        out_specs=[VMEM] * 3,
        out_shape=[stat, stat, jax.ShapeDtypeStruct((2, 16, 128), BF16)],
        scratch_shapes=[pltpu.VMEM((8, 128, 128), F32)],
        compiler_params=params(24),
        name="merge",
        cost_estimate=pl.CostEstimate(flops=1 << 26, bytes_accessed=2 << 20, transcendentals=1 << 17),
    )(col[None].astype(jnp.int32), parts, pooled, w_token_out, w_back)
    near = lax.ppermute(low[0], "col", core_pairs)
    far = lax.ppermute(low[0], ("row", "col"), chip_pairs)

    pair_grad = pl.pallas_call(
        pair_grad_kernel,
        grid=(steps,),
        in_specs=[
            pl.BlockSpec((16 // steps, HT, GROUP, 256), lambda i: (i, 0, 0, 0)),
            pl.BlockSpec((16 // steps, HT, GROUP, 256), lambda i: (i, 0, 0, 0)),
            pl.BlockSpec((128 // steps, 128), lambda i: (i, 0)),
            pl.BlockSpec((128 // steps, 128), lambda i: (i, 0)),
            pl.BlockSpec((128, 128), lambda i: (0, 0)),
        ],
        out_specs=pl.BlockSpec((128 // steps, 256, 128), lambda i: (i, 0, 0)),
        out_shape=jax.ShapeDtypeStruct((128, 256, 128), BF16),
        compiler_params=params(32),
        name="pair_grad",
        cost_estimate=pl.CostEstimate(
            flops=2 * 128 * 256 * 128 * 16 * 8, bytes_accessed=14 << 20, transcendentals=0
        ),
    )(prob, grad, scale, diag, head_rows)
    atom_out = pl.pallas_call(
        atom_out_kernel,
        in_specs=[SMEM] + [VMEM] * 5,
        out_specs=VMEM,
        out_shape=jax.ShapeDtypeStruct((128, 128), BF16),
        name="atom_out",
        cost_estimate=pl.CostEstimate(flops=1 << 21, bytes_accessed=1 << 17, transcendentals=0),
    )(flags, near, far, low, aux, hidden)
    return (atom_out, pair_grad.reshape(pair.shape))


def solution(mesh):
    return jax.shard_map(
        shards,
        mesh=mesh,
        in_specs=(
            P(("row", "col"), None),
            P(None, ("row", "col"), None),
            P(("row", "col")),
            P(("row", "col")),
            P(("row", "col")),
            P(("row", "col")),
            P("row", None, "col", None, None),
            P(),
            P(),
            P(),
            P(),
            P(),
            P(),
            P(),
            P(("row", "col"), None),
        ),
        out_specs=(P(("row", "col"), None), P("row", None, "col", None, None)),
        check_vma=False,
    )
```

```python
import functools
import math

import jax
import jax.numpy as jnp
from jax import lax
from jax.experimental import pallas as pl
from jax.experimental.pallas import tpu as pltpu
from jax.sharding import PartitionSpec as P

HA = 4
HT = 16
QB = 32
KW = 128
SHIFT = 16
HALF = 64
EARLY = 8
GROUP = 8
AUX = 16
EPSILON = 1e-05
LOWEST = -1e30
F32 = jnp.float32
BF16 = jnp.bfloat16
NT = (((1,), (1,)), ((), ()))
TN = (((0,), (0,)), ((), ()))

VMEM = pl.BlockSpec(memory_space=pltpu.VMEM)
HBM = pl.BlockSpec(memory_space=pltpu.HBM)
SMEM = pl.BlockSpec(memory_space=pltpu.SMEM)


def params(mib):
    return pltpu.CompilerParams(vmem_limit_bytes=mib << 20)


def outside(value):
    return pltpu.with_memory_space_constraint(value, pltpu.HBM)


def inside(value):
    return pltpu.with_memory_space_constraint(value, pltpu.VMEM)


def place():
    return lax.axis_index("row"), lax.axis_index("col")


def iota(shape, dim):
    return lax.broadcasted_iota(jnp.int32, shape, dim)


def dot(a, b, dims=None):
    if dims is None:
        return jnp.dot(a, b, preferred_element_type=F32)
    return lax.dot_general(a, b, dims, preferred_element_type=F32)


def normal(values):
    centred = values - jnp.mean(values, axis=-1, keepdims=True)
    return centred * lax.rsqrt(jnp.mean(centred * centred, axis=-1, keepdims=True) + EPSILON)


def split(values):
    high = values.astype(BF16)
    return high, (values - high.astype(F32)).astype(BF16)


def grouped_weight(head_rows, member):
    rows = iota(head_rows.shape, 0)
    return jnp.where(rows % GROUP == member, head_rows, 0.0).astype(BF16)


def pair_bias_kernel(first, pair_ref, head_ref, out_ref, tile_ref, arrived):
    groups = out_ref.shape[0]
    window = min(8, groups)

    def copy(g):
        rows = pl.ds(g * GROUP, GROUP)
        here = pl.ds((g + first) * GROUP, GROUP)
        return pltpu.make_async_copy(pair_ref.at[here], tile_ref.at[rows], arrived.at[g])

    for g in range(window):
        copy(g).start()
    weight = head_ref[...].astype(F32).reshape(HT, GROUP, 128)[:, 0].astype(BF16)

    def step(g, carry):
        copy(g).wait()
        if window < groups:

            @pl.when(g + window < groups)
            def _():
                copy(g + window).start()

        for i in range(GROUP):
            out_ref[g, :, i, :] = dot(weight, tile_ref[g * GROUP + i], NT)
        return carry

    lax.fori_loop(0, groups, step, 0)


def pack_kernel(shift_ref, atoms_ref, bias_ref, cot_ref, token_ref, near_ref, far_ref):
    row, col = place()
    odd = lax.rem(col, 2)
    line = iota((AUX, 128), 0)
    device = row * lax.axis_size("col") + col
    aux = jnp.where(line == 0, token_ref[...] - (16 * device - 17), 0)
    for n in range(4):
        aux = jnp.where(line == 1 + n, shift_ref[n], aux)
    aux = aux.astype(F32).astype(BF16)

    def fill(out_ref, at):
        out_ref[0:128] = atoms_ref[...]
        for h in range(HA):
            out_ref[128 + HALF * h : 128 + HALF * (h + 1)] = bias_ref[h, at : at + HALF]
        out_ref[384:448] = cot_ref[at : at + HALF]
        out_ref[448:464] = aux

    @pl.when(odd == 1)
    def _():
        fill(near_ref, 0)
        fill(far_ref, HALF)

    @pl.when(odd == 0)
    def _():
        fill(near_ref, HALF)
        fill(far_ref, 0)


def atom_kernel(
    shift_ref,
    count_ref,
    mask_ref,
    near_ref,
    far_ref,
    atoms_ref,
    bias_ref,
    cot_ref,
    token_ref,
    after_ref,
    w_qkv_ref,
    w_out_ref,
    w_pool_ref,
    token_out_ref,
    back_ref,
    hidden_ref,
    pooled_ref,
    to_row_ref,
    to_col_ref,
    inner_out_ref,
    inner_back_ref,
    prev_ref,
    next_ref,
    arrived,
):
    pairs = (
        (token_out_ref, inner_out_ref),
        (back_ref, inner_back_ref),
    )
    copies = [pltpu.make_async_copy(a, b, arrived.at[n]) for n, (a, b) in enumerate(pairs)]
    for copy in copies:
        copy.start()
    row, col = place()
    odd = lax.rem(col, 2)
    device = row * lax.axis_size("col") + col
    atom_count = 128 * lax.axis_size("row") * lax.axis_size("col")

    @pl.when(odd == 1)
    def _():
        prev_ref[...] = near_ref[...]
        next_ref[...] = far_ref[...]

    @pl.when(odd == 0)
    def _():
        prev_ref[...] = far_ref[...]
        next_ref[...] = near_ref[...]

    first = device * 128
    extended = jnp.concatenate([prev_ref[0:128], atoms_ref[...], next_ref[0:128]], axis=0)
    wide = extended.astype(F32)
    project = dot(normal(wide).astype(BF16), w_qkv_ref[...]).astype(BF16)
    head_lane = iota((QB, 128), 1) // 32
    head_mask = [jnp.where(head_lane == h, 1.0, 0.0) for h in range(HA)]
    slot = iota((1, KW), 1)
    offset = iota((KW, 160), 1) - iota((KW, 160), 0) - SHIFT
    order = (2, 3, 4, 5, 6, 7, 0, 1)
    biases, shifts, windows, stacks = [], [], [], []
    for block in order:
        if block < 2:
            source, local = prev_ref, block
            shift = prev_ref[451 + local : 452 + local].astype(F32).astype(jnp.int32)
        elif block > 5:
            source, local = next_ref, block - 6
            shift = next_ref[449 + local : 450 + local].astype(F32).astype(jnp.int32)
        else:
            source, local = None, block - 2
            shift = jnp.full((1, 128), shift_ref[local], jnp.int32)
        for h in range(HA):
            if source is None:
                biases.append(bias_ref[h, 32 * local : 32 * local + 32])
            else:
                at = 128 + HALF * h + 32 * local
                biases.append(source[at : at + 32])
        shifts.append(shift)
    for block, shift in zip(order, shifts):
        pick = jnp.where(offset == shift[:, 0:1], 1.0, 0.0).astype(BF16)
        windows.append(dot(pick, project[32 * block : 32 * block + 160, 128:]).astype(BF16))
        query = project[64 + 32 * block : 96 + 32 * block, :128].astype(F32)
        stacks.append(
            jnp.concatenate([query * head_mask[h] for h in range(HA)], axis=0).astype(BF16)
        )
    scores = [
        dot(stack, window[:, :128], NT) * (1.0 / math.sqrt(32))
        for stack, window in zip(stacks, windows)
    ]
    weights = []
    for n, block in enumerate(order):
        score = scores[n] + jnp.concatenate(biases[HA * n : HA * n + HA], axis=0).astype(F32)
        position = slot + (first + 32 * block - 112) + shifts[n]
        inside = (position >= 0) & (position < atom_count)
        score = jnp.where(inside, score, LOWEST)
        raised = jnp.exp(score - jnp.max(score, axis=-1, keepdims=True))
        weights.append((raised / jnp.sum(raised, axis=-1, keepdims=True)).astype(BF16))
    mixes = []
    for weight, window in zip(weights, windows):
        mixed = dot(weight, window[:, 128:])
        mix = mixed[0:32] * head_mask[0]
        for h in range(1, HA):
            mix = mix + mixed[32 * h : 32 * h + 32] * head_mask[h]
        mixes.append(mix)
    mixture = jnp.concatenate(mixes, axis=0).astype(BF16)
    base = jnp.concatenate([wide[128:320], wide[64:128]], axis=0)
    hidden = (base + dot(mixture, w_out_ref[...])).astype(BF16)
    hidden_ref[...] = hidden[:128]
    lifted = jnp.maximum(dot(hidden, w_pool_ref[...]), 0.0)
    own_token = (token_ref[...] - 16 * device).astype(F32)
    prev_token = prev_ref[448:449].astype(F32) - 33.0
    next_token = next_ref[448:449].astype(F32) - 1.0
    beside = jnp.where(iota((1, 128), 1) < HALF, next_token, prev_token)
    token = jnp.concatenate([own_token, beside], axis=1)
    select = jnp.where(iota((16, 256), 0).astype(F32) == token, 1.0, 0.0).astype(BF16)
    high, low = split(lifted)
    line = iota((16, 128), 0)
    count = jnp.zeros((16, 128), jnp.int32)
    live = jnp.zeros((16, 128), jnp.int32)
    for t in range(16):
        count = jnp.where(line == t, count_ref[t], count)
        live = jnp.where(line == t, mask_ref[t], live)
    count = jnp.concatenate([count.astype(F32)] * 6, axis=1)
    pooled = (dot(select, high) + dot(select, low)) / count
    pooled_ref[...] = pooled
    normed = normal(pooled).astype(BF16)
    cot = jnp.concatenate([cot_ref[...], next_ref[384:448], prev_ref[384:448]], axis=0)
    grad_up = dot(select, cot).astype(BF16)
    live = live.astype(F32).astype(BF16)
    for r in range(to_row_ref.shape[0]):
        to_row_ref[r, :, :768] = normed
        to_row_ref[r, :, 768:] = live
    to_col_ref[:, :768] = normed
    to_col_ref[:, 768:] = grad_up
    for copy in copies:
        copy.wait()


def window_of(head):
    block, rest = divmod(head, 8)
    return 384 * block + (0 if rest < 5 else 128)


def stack_kernel(first_ref, second_ref, third_ref, fourth_ref, out_ref):
    for n, part in enumerate((first_ref, second_ref, third_ref, fourth_ref)):
        out_ref[n] = part[...]


def token_kernel(
    keys_ref,
    own_ref,
    partner_ref,
    early_ref,
    late_ref,
    w_qkv_ref,
    w_out_ref,
    w_back_ref,
    prob_ref,
    grad_ref,
    stats_ref,
    keep_ref,
    give_ref,
    rows_ref,
    inner_ref,
    mixed_ref,
    arrived,
):
    copies = []
    for n in range(6):
        rows = slice(128 * n, 128 * (n + 1))
        copies.append(
            pltpu.make_async_copy(w_qkv_ref.at[rows], inner_ref.at[rows], arrived.at[n])
        )
    for copy in copies:
        copy.start()
    row, col = place()
    chip, core = lax.div(col, 2), lax.rem(col, 2)
    for s in range(4):
        there = lax.rem(chip + 4 - s, 4) * 32
        rows_ref[pl.ds(pl.multiple_of(there + core * 16, 16), 16)] = own_ref[s]
        rows_ref[pl.ds(pl.multiple_of(there + 16 - core * 16, 16), 16)] = partner_ref[s]
    middle = dot(rows_ref[:, 768:], w_back_ref[...], NT).astype(BF16)
    grad = dot(middle, w_out_ref[...], NT).astype(BF16)
    for copy in copies:
        copy.wait()
    query = dot(rows_ref[:, :768], inner_ref[:, :768]).astype(BF16)
    key = dot(keys_ref[:, :768], inner_ref[:, 768:1536]).astype(BF16)
    value = dot(keys_ref[:, :768], inner_ref[:, 1536:]).astype(BF16)
    live = keys_ref[:, 768:].astype(F32).T[0:1]
    closed = jnp.where(live > 0, 0.0, -jnp.inf)
    lane = iota((128, 256), 1)
    stat_lane = iota((128, 128), 1)

    def within(h):
        at = window_of(h)
        return (lane >= 48 * h - at) & (lane < 48 * (h + 1) - at)

    for h in range(HT):
        at = window_of(h)
        query_h = jnp.where(within(h), query[:, at : at + 256].astype(F32), 0.0).astype(BF16)
        scores = dot(query_h, key[:, at : at + 256], NT) * (1.0 / math.sqrt(48))
        bias = jnp.concatenate([early_ref[:, h], late_ref[:, h]], axis=0).reshape(128, 256)
        prob_ref[:, h] = (scores + bias + closed).reshape(16, GROUP, 256)
    for h in range(HT):
        at = window_of(h)
        grad_h = jnp.where(within(h), grad[:, at : at + 256].astype(F32), 0.0).astype(BF16)
        grads = dot(grad_h, value[:, at : at + 256], NT)
        grad_ref[:, h] = grads.reshape(16, GROUP, 256)
    tops = jnp.zeros((128, 128), F32)
    sums = jnp.zeros((128, 128), F32)
    diags = jnp.zeros((128, 128), F32)
    for h in range(HT):
        scores = prob_ref[:, h].reshape(128, 256)
        top = jnp.maximum(jnp.max(scores, axis=-1, keepdims=True), LOWEST)
        high = top.astype(BF16).astype(F32)
        top = high + (top - high).astype(BF16).astype(F32)
        raised = jnp.exp(scores - top)
        prob_ref[:, h] = raised.reshape(16, GROUP, 256)
        total = jnp.sum(raised, axis=-1, keepdims=True)
        diag = jnp.sum(raised * grad_ref[:, h].reshape(128, 256), axis=-1, keepdims=True)
        here = stat_lane == h
        tops = jnp.where(here, top, tops)
        sums = jnp.where(here, total, sums)
        diags = jnp.where(here, diag, diags)
    for at in (0, 128, 384, 512):
        out = None
        for h in range(HT):
            if window_of(h) == at:
                raised = prob_ref[:, h].reshape(128, 256).astype(BF16)
                part = jnp.where(within(h), dot(raised, value[:, at : at + 256]), 0.0)
                out = part if out is None else out + part
        if at % 384 == 0:
            mixed_ref[:, at : at + 256] = out
        else:
            mixed_ref[:, at : at + 128] = mixed_ref[:, at : at + 128] + out[:, :128]
            mixed_ref[:, at + 128 : at + 256] = out[:, 128:]
    stats_ref[...] = tops + pltpu.roll(sums, 32, axis=1) + pltpu.roll(diags, 64, axis=1)
    packed = packed_stats(tops, sums, diags)
    for n in range(4):
        there = 32 * n + 16 * core
        keep_ref[n] = mixed_ref[pl.ds(pl.multiple_of(there, 16), 16)]
        there = 32 * n + 16 - 16 * core
        part = mixed_ref[pl.ds(pl.multiple_of(there, 16), 16)]
        give_ref[n, :, :768] = part.astype(BF16)
        for k in range(2):
            at = 32 * n + 16 * k
            give_ref[n, :, 768 + 128 * k : 896 + 128 * k] = packed[at : at + 16]


def packed_stats(tops, sums, diags):
    stats = jnp.zeros((128, 128), F32)
    for k, part in enumerate((tops, sums, diags)):
        high = part.astype(BF16).astype(F32)
        for n, piece in enumerate((high, part - high)):
            turn = 32 * k + 16 * n
            stats = stats + (pltpu.roll(piece, turn, axis=1) if turn else piece)
    return stats.astype(BF16)


def spread_heads(factors):
    spread = jnp.where(iota((128, 768), 1) // 48 == iota((128, 768), 0), 1.0, 0.0).astype(BF16)
    high, low = split(factors)
    return dot(high, spread) + dot(low, spread)


def parted_stats(stats):
    lane = iota((128, 128), 1)
    parts = [stats, pltpu.roll(stats, 96, axis=1), pltpu.roll(stats, 64, axis=1)]
    return [jnp.where(lane < HT, part, 0.0) for part in parts]


def fold_kernel(
    keep_ref,
    stats_ref,
    given_ref,
    first_ref,
    second_ref,
    third_ref,
    own_ref,
    joint_ref,
    ratio_ref,
    mixed_ref,
):
    row, col = place()
    chip, core = lax.div(col, 2), lax.rem(col, 2)
    given = jnp.concatenate(
        [given_ref[n, :, 768 + 128 * k : 896 + 128 * k] for n in range(4) for k in range(2)],
        axis=0,
    ).astype(F32)
    given = given + pltpu.roll(given, 112, axis=1)
    sides = [parted_stats(stats_ref[...]), parted_stats(given)]
    top = jnp.maximum(sides[0][0], sides[1][0])
    ratios = [jnp.exp(side[0] - top) for side in sides]
    total = ratios[0] * sides[0][1] + ratios[1] * sides[1][1]
    diag = ratios[0] * sides[0][2] + ratios[1] * sides[1][2]
    joint_ref[...] = top + pltpu.roll(total, 32, axis=1) + pltpu.roll(diag, 64, axis=1)
    ratio_ref[0] = ratios[0]
    ratio_ref[1] = ratios[1]
    rows = [pl.ds(pl.multiple_of(32 * n + 16 * core, 16), 16) for n in range(4)]
    factors = spread_heads(
        jnp.concatenate([ratio_ref[side, rows[n]] for side in range(2) for n in range(4)], axis=0)
    )
    for n in range(4):
        given_n = given_ref[n, :, :768].astype(F32)
        mixed_ref[n] = (
            keep_ref[n] * factors[16 * n : 16 * n + 16]
            + given_n * factors[64 + 16 * n : 80 + 16 * n]
        )
    packed = packed_stats(top, total, diag)
    for s, out_ref in enumerate((first_ref, second_ref, third_ref)):
        out_ref[:, :768] = mixed_ref[lax.rem(chip + s + 1, 4)].astype(BF16)
        for k in range(8):
            out_ref[:, 768 + 128 * k : 896 + 128 * k] = packed[16 * k : 16 * k + 16]
    own_ref[...] = mixed_ref[chip]


def merge_kernel(
    stats_ref,
    own_ref,
    joint_ref,
    first_ref,
    second_ref,
    third_ref,
    pooled_ref,
    w_out_ref,
    w_back_ref,
    scale_ref,
    diag_ref,
    low_ref,
    ratio_ref,
):
    row, col = place()
    lane = iota((128, 128), 1)
    sides = [parted_stats(joint_ref[...])]
    for part_ref in (first_ref, second_ref, third_ref):
        stats = jnp.concatenate(
            [part_ref[:, 768 + 128 * k : 896 + 128 * k] for k in range(8)], axis=0
        ).astype(F32)
        sides.append(parted_stats(stats + pltpu.roll(stats, 112, axis=1)))
    top = functools.reduce(jnp.maximum, [side[0] for side in sides])
    ratios = [jnp.exp(side[0] - top) for side in sides]
    total = functools.reduce(jnp.add, [r * side[1] for r, side in zip(ratios, sides)])
    diag = functools.reduce(jnp.add, [r * side[2] for r, side in zip(ratios, sides)])
    inverse = 1.0 / jnp.where(lane < HT, total, 1.0)
    for n in range(4):
        ratio_ref[n] = ratios[n] * inverse
    own_top = parted_stats(stats_ref[...])[0]
    scale_ref[...] = jnp.exp(own_top - top) * inverse
    diag_ref[...] = diag * inverse
    rows = pl.ds(pl.multiple_of(col * 16, 16), 16)
    factors = spread_heads(jnp.concatenate([ratio_ref[n, rows] for n in range(4)], axis=0))
    mixed = own_ref[...] * factors[0:16]
    for n, part_ref in enumerate((first_ref, second_ref, third_ref)):
        mixed = mixed + part_ref[:, :768].astype(F32) * factors[16 * n + 16 : 16 * n + 32]
    updated = (pooled_ref[...] + dot(mixed.astype(BF16), w_out_ref[...])).astype(BF16)
    high, low = split(dot(updated, w_back_ref[...]))
    low_ref[0] = high
    low_ref[1] = low


def pair_grad_kernel(prob_ref, grad_ref, scale_ref, diag_ref, head_ref, out_ref, tile_ref, left):
    groups = prob_ref.shape[0]

    def copy(g):
        rows = pl.ds(g * GROUP, GROUP)
        return pltpu.make_async_copy(tile_ref.at[rows], out_ref.at[rows], left.at[g])

    head_rows = head_ref[...].astype(F32)
    weights = jnp.concatenate([grouped_weight(head_rows, i) for i in range(GROUP)], axis=1)

    def score_of(g):
        rows = pl.ds(pl.multiple_of(g * GROUP, GROUP), GROUP)
        scale = scale_ref[rows]
        diag = diag_ref[rows]
        score = jnp.concatenate(
            [
                prob_ref[g, h] * scale[:, h : h + 1] * (grad_ref[g, h] - diag[:, h : h + 1])
                for h in range(HT)
            ],
            axis=0,
        )
        return score.T.astype(BF16)

    def step(g, score):
        following = score_of(jnp.minimum(g + 1, groups - 1))
        result = dot(score, weights)
        for i in range(GROUP):
            tile_ref[g * GROUP + i] = result[:, 128 * i : 128 * (i + 1)].astype(BF16)
        copy(g).start()
        return following

    lax.fori_loop(0, groups, step, score_of(0), unroll=2)
    for g in range(groups):
        copy(g).wait()


def atom_out_kernel(near_ref, far_ref, low_ref, token_ref, hidden_ref, out_ref):
    row, col = place()
    odd = lax.rem(col, 2) == 1
    device = row * lax.axis_size("col") + col
    near = near_ref[...].astype(F32)
    far = far_ref[...].astype(F32)
    before = jnp.where(odd, near, far).astype(BF16)
    after = jnp.where(odd, far, near).astype(BF16)
    rows = jnp.concatenate([before, low_ref[0], after, low_ref[1]], axis=0)
    token = (token_ref[...] - (16 * device - 16)).astype(F32)
    index = iota((64, 128), 0)
    index = jnp.where(index < 48, index, index - 32).astype(F32)
    select = jnp.where(index == token, 1.0, 0.0).astype(BF16)
    out_ref[...] = (hidden_ref[...].astype(F32) + dot(select, rows, TN)).astype(BF16)


def shards(
    atoms,
    atom_bias,
    key_shift,
    atom_token,
    token_atoms,
    token_mask,
    pair,
    w_atom_qkv,
    w_atom_out,
    w_pool,
    w_token_qkv,
    w_token_out,
    w_bias,
    w_back,
    cotangent,
):
    row_count, col_count = lax.axis_size("row"), lax.axis_size("col")
    devices = row_count * col_count
    core_pairs = [(i, i ^ 1) for i in range(col_count)]
    chip_pairs = [(i, i + 1) for i in range(1, devices - 1, 2)]
    chip_pairs = chip_pairs + [(j, i) for i, j in chip_pairs]

    def chip_shift(steps):
        return [(i, (i + 2 * steps) % col_count) for i in range(col_count)]

    tokens = atom_token.reshape(1, 128)
    payload = jax.ShapeDtypeStruct((464, 128), BF16)
    near, far = pl.pallas_call(
        pack_kernel,
        in_specs=[SMEM] + [VMEM] * 4,
        out_specs=[VMEM, VMEM],
        out_shape=[payload, payload],
        compiler_params=params(4),
        name="pack",
        cost_estimate=pl.CostEstimate(flops=0, bytes_accessed=1 << 20, transcendentals=0),
    )(
        outside(key_shift),
        outside(atoms),
        outside(atom_bias),
        outside(cotangent),
        outside(tokens),
    )
    near = lax.ppermute(near, "col", core_pairs)
    far = lax.ppermute(far, ("row", "col"), chip_pairs)

    tile = pair.reshape(128, 256, 128)
    head_rows = jnp.repeat(jnp.transpose(w_bias), GROUP, axis=0)
    def pair_bias(first, groups, name):
        return pl.pallas_call(
            functools.partial(pair_bias_kernel, first),
            in_specs=[HBM, VMEM],
            out_specs=VMEM,
            out_shape=pltpu.VMEM((groups, HT, GROUP, 256), F32),
            scratch_shapes=[
                pltpu.VMEM((groups * GROUP, 256, 128), BF16),
                pltpu.SemaphoreType.DMA((groups,)),
            ],
            compiler_params=params(14),
            name=name,
            cost_estimate=pl.CostEstimate(
                flops=groups << 26, bytes_accessed=groups << 19, transcendentals=0
            ),
        )(outside(tile), head_rows)

    half = EARLY
    early = pair_bias(0, half, "pair_bias_early")
    late = pair_bias(half, 16 - half, "pair_bias_late")

    hidden, pooled, to_row, to_col, token_out, back = pl.pallas_call(
        atom_kernel,
        in_specs=[SMEM] * 3 + [VMEM] * 6 + [pl.BlockSpec(memory_space=pl.ANY)] + [VMEM] * 3 + [HBM] * 2,
        out_specs=[VMEM] * 6,
        out_shape=[
            pltpu.VMEM((128, 128), BF16),
            pltpu.HBM((16, 768), F32),
            pltpu.HBM((row_count, 16, 896), BF16),
            pltpu.HBM((16, 896), BF16),
            pltpu.VMEM(w_token_out.shape, BF16),
            pltpu.VMEM(w_back.shape, BF16),
        ],
        scratch_shapes=[
            pltpu.VMEM((464, 128), BF16),
            pltpu.VMEM((464, 128), BF16),
            pltpu.SemaphoreType.DMA((2,)),
        ],
        compiler_params=params(8),
        name="atom_stage",
        cost_estimate=pl.CostEstimate(flops=1 << 28, bytes_accessed=2 << 20, transcendentals=1 << 17),
    )(
        outside(key_shift),
        outside(token_atoms),
        outside(token_mask),
        near,
        far,
        outside(atoms),
        outside(atom_bias),
        outside(cotangent),
        outside(tokens),
        inside(early),
        outside(w_atom_qkv),
        outside(w_atom_out),
        outside(w_pool),
        outside(w_token_out),
        outside(w_back),
    )
    shifted = [lax.ppermute(to_col, "col", chip_shift(s)) for s in range(1, 4)]
    keys = lax.all_to_all(to_row, "row", 0, 0).reshape(256, 896)
    own = pl.pallas_call(
        stack_kernel,
        in_specs=[VMEM] * 4,
        out_specs=VMEM,
        out_shape=pltpu.HBM((4, 16, 896), BF16),
        compiler_params=params(4),
        name="stack",
        cost_estimate=pl.CostEstimate(flops=1 << 32, bytes_accessed=1 << 18, transcendentals=0),
    )(outside(to_col), *shifted)
    partner = lax.ppermute(own, "col", core_pairs)

    stat = pltpu.VMEM((128, 128), F32)
    swapped = jax.ShapeDtypeStruct((4, 16, 1024), BF16)
    folded = jax.ShapeDtypeStruct((16, 1792), BF16)
    table = pltpu.VMEM((16, HT, GROUP, 256), F32)
    prob, grad, stats, keep, give = pl.pallas_call(
        token_kernel,
        in_specs=[VMEM] * 5 + [HBM] + [VMEM] * 2,
        out_specs=[VMEM] * 5,
        scratch_shapes=[
            pltpu.VMEM((128, 896), BF16),
            pltpu.VMEM((768, 2304), BF16),
            pltpu.VMEM((128, 768), F32),
            pltpu.SemaphoreType.DMA((6,)),
        ],
        out_shape=[table, table, stat, pltpu.VMEM((4, 16, 768), F32), swapped],
        compiler_params=params(16),
        name="token_stage",
        cost_estimate=pl.CostEstimate(flops=1 << 31, bytes_accessed=12 << 20, transcendentals=1 << 19),
    )(
        outside(keys),
        outside(own),
        outside(partner),
        inside(early),
        inside(late),
        outside(w_token_qkv),
        inside(token_out),
        inside(back),
    )
    given = lax.ppermute(give, "col", core_pairs)
    *sent, mixed, joint = pl.pallas_call(
        fold_kernel,
        in_specs=[VMEM] * 3,
        out_specs=[VMEM] * 5,
        out_shape=[folded, folded, folded, pltpu.VMEM((16, 768), F32), stat],
        scratch_shapes=[pltpu.VMEM((2, 128, 128), F32), pltpu.VMEM((4, 16, 768), F32)],
        compiler_params=params(6),
        name="fold",
        cost_estimate=pl.CostEstimate(flops=1 << 26, bytes_accessed=2 << 20, transcendentals=1 << 17),
    )(inside(keep), inside(stats), given)
    parts = [lax.ppermute(part, "col", chip_shift(s + 1)) for s, part in enumerate(sent)]

    scale, diag, low = pl.pallas_call(
        merge_kernel,
        in_specs=[VMEM] * 9,
        out_specs=[VMEM] * 3,
        out_shape=[stat, stat, pltpu.VMEM((2, 16, 128), BF16)],
        scratch_shapes=[pltpu.VMEM((4, 128, 128), F32)],
        compiler_params=params(6),
        name="merge",
        cost_estimate=pl.CostEstimate(flops=1 << 26, bytes_accessed=2 << 20, transcendentals=1 << 17),
    )(
        inside(stats),
        inside(mixed),
        inside(joint),
        *parts,
        outside(pooled),
        inside(token_out),
        inside(back),
    )
    near = lax.ppermute(low[0], "col", core_pairs)
    far = lax.ppermute(low[0], ("row", "col"), chip_pairs)

    pair_grad = pl.pallas_call(
        pair_grad_kernel,
        in_specs=[VMEM] * 5,
        out_specs=HBM,
        out_shape=jax.ShapeDtypeStruct((128, 256, 128), BF16),
        scratch_shapes=[pltpu.VMEM((128, 256, 128), BF16), pltpu.SemaphoreType.DMA((16,))],
        compiler_params=params(14),
        name="pair_grad",
        cost_estimate=pl.CostEstimate(
            flops=2 * 128 * 256 * 128 * 16 * 8, bytes_accessed=14 << 20, transcendentals=0
        ),
    )(inside(prob), inside(grad), inside(scale), inside(diag), head_rows)
    atom_out = pl.pallas_call(
        atom_out_kernel,
        in_specs=[VMEM] * 5,
        out_specs=VMEM,
        out_shape=jax.ShapeDtypeStruct((128, 128), BF16),
        compiler_params=params(4),
        name="atom_out",
        cost_estimate=pl.CostEstimate(flops=1 << 21, bytes_accessed=1 << 17, transcendentals=0),
    )(near, far, inside(low), outside(tokens), inside(hidden))
    return (atom_out, pair_grad.reshape(pair.shape))


def solution(mesh):
    return jax.shard_map(
        shards,
        mesh=mesh,
        in_specs=(
            P(("row", "col"), None),
            P(None, ("row", "col"), None),
            P(("row", "col")),
            P(("row", "col")),
            P(("row", "col")),
            P(("row", "col")),
            P("row", None, "col", None, None),
            P(),
            P(),
            P(),
            P(),
            P(),
            P(),
            P(),
            P(("row", "col"), None),
        ),
        out_specs=(P(("row", "col"), None), P("row", None, "col", None, None)),
        check_vma=False,
    )
```

```python
import functools
import math

import jax
import jax.numpy as jnp
from jax import lax
from jax.experimental import pallas as pl
from jax.experimental.pallas import tpu as pltpu
from jax.sharding import PartitionSpec as P

HA = 4
HT = 16
QB = 32
KW = 128
SHIFT = 16
HALF = 64
EARLY = 8
GROUP = 8
AUX = 16
EPSILON = 1e-05
LOWEST = -1e30
MASKED = 1024.0
F32 = jnp.float32
BF16 = jnp.bfloat16
NT = (((1,), (1,)), ((), ()))
TN = (((0,), (0,)), ((), ()))

VMEM = pl.BlockSpec(memory_space=pltpu.VMEM)
HBM = pl.BlockSpec(memory_space=pltpu.HBM)
SMEM = pl.BlockSpec(memory_space=pltpu.SMEM)


def params(mib):
    return pltpu.CompilerParams(vmem_limit_bytes=mib << 20)


def outside(value):
    return pltpu.with_memory_space_constraint(value, pltpu.HBM)


def inside(value):
    return pltpu.with_memory_space_constraint(value, pltpu.VMEM)


def place():
    return lax.axis_index("row"), lax.axis_index("col")


def iota(shape, dim):
    return lax.broadcasted_iota(jnp.int32, shape, dim)


def dot(a, b, dims=None):
    if dims is None:
        return jnp.dot(a, b, preferred_element_type=F32)
    return lax.dot_general(a, b, dims, preferred_element_type=F32)


def normal(values):
    centred = values - jnp.mean(values, axis=-1, keepdims=True)
    return centred * lax.rsqrt(jnp.mean(centred * centred, axis=-1, keepdims=True) + EPSILON)


def split(values):
    high = values.astype(BF16)
    return high, (values - high.astype(F32)).astype(BF16)


def grouped_weight(head_rows, member):
    rows = iota(head_rows.shape, 0)
    return jnp.where(rows % GROUP == member, head_rows, 0.0).astype(BF16)


def pair_bias_kernel(
    first, pair_ref, head_ref, out_ref, tile_ref, bias_ref, arrived, left
):
    groups = out_ref.shape[0]
    window = min(8, groups)

    def copy(g):
        rows = pl.ds(g * GROUP, GROUP)
        here = pl.ds((g + first) * GROUP, GROUP)
        return pltpu.make_async_copy(pair_ref.at[here], tile_ref.at[rows], arrived.at[g])

    def leave(g):
        return pltpu.make_async_copy(bias_ref.at[g], out_ref.at[g], left.at[g])

    for g in range(window):
        copy(g).start()
    weight = head_ref[...].astype(F32).reshape(HT, GROUP, 128)[:, 0].astype(BF16)

    def step(g, carry):
        copy(g).wait()
        if window < groups:

            @pl.when(g + window < groups)
            def _():
                copy(g + window).start()

        for i in range(GROUP):
            bias_ref[g, :, i, :] = dot(weight, tile_ref[g * GROUP + i], NT)
        leave(g).start()
        return carry

    lax.fori_loop(0, groups, step, 0)
    for g in range(groups):
        leave(g).wait()


def pack_kernel(shift_ref, atoms_ref, bias_ref, cot_ref, token_ref, near_ref, far_ref):
    row, col = place()
    odd = lax.rem(col, 2)
    line = iota((AUX, 128), 0)
    device = row * lax.axis_size("col") + col
    aux = jnp.where(line == 0, token_ref[...] - (16 * device - 17), 0)
    for n in range(4):
        aux = jnp.where(line == 1 + n, shift_ref[n], aux)
    aux = aux.astype(F32).astype(BF16)

    def fill(out_ref, at):
        out_ref[0:128] = atoms_ref[...]
        for h in range(HA):
            out_ref[128 + HALF * h : 128 + HALF * (h + 1)] = bias_ref[h, at : at + HALF]
        out_ref[384:448] = cot_ref[at : at + HALF]
        out_ref[448:464] = aux

    @pl.when(odd == 1)
    def _():
        fill(near_ref, 0)
        fill(far_ref, HALF)

    @pl.when(odd == 0)
    def _():
        fill(near_ref, HALF)
        fill(far_ref, 0)


def atom_kernel(
    shift_ref,
    count_ref,
    mask_ref,
    near_ref,
    far_ref,
    atoms_ref,
    bias_ref,
    cot_ref,
    token_ref,
    after_ref,
    w_qkv_ref,
    w_out_ref,
    w_pool_ref,
    token_qkv_ref,
    hidden_ref,
    pooled_ref,
    to_row_ref,
    to_col_ref,
    token_kv_ref,
    prev_ref,
    next_ref,
    arrived,
):
    copies = []
    for n in range(4):
        rows = slice(192 * n, 192 * (n + 1))
        copies.append(
            pltpu.make_async_copy(
                token_qkv_ref.at[rows, 768:2304], token_kv_ref.at[rows], arrived.at[n]
            )
        )
    for copy in copies:
        copy.start()
    row, col = place()
    odd = lax.rem(col, 2)
    device = row * lax.axis_size("col") + col
    atom_count = 128 * lax.axis_size("row") * lax.axis_size("col")

    @pl.when(odd == 1)
    def _():
        prev_ref[...] = near_ref[...]
        next_ref[...] = far_ref[...]

    @pl.when(odd == 0)
    def _():
        prev_ref[...] = far_ref[...]
        next_ref[...] = near_ref[...]

    first = device * 128
    extended = jnp.concatenate([prev_ref[0:128], atoms_ref[...], next_ref[0:128]], axis=0)
    wide = extended.astype(F32)
    project = dot(normal(wide).astype(BF16), w_qkv_ref[...]).astype(BF16)
    head_lane = iota((QB, 128), 1) // 32
    head_mask = [jnp.where(head_lane == h, 1.0, 0.0) for h in range(HA)]
    slot = iota((1, KW), 1)
    offset = iota((KW, 160), 1) - iota((KW, 160), 0) - SHIFT
    order = (2, 3, 4, 5, 6, 7, 0, 1)
    biases, shifts, windows, stacks = [], [], [], []
    for block in order:
        if block < 2:
            source, local = prev_ref, block
            shift = prev_ref[451 + local : 452 + local].astype(F32).astype(jnp.int32)
        elif block > 5:
            source, local = next_ref, block - 6
            shift = next_ref[449 + local : 450 + local].astype(F32).astype(jnp.int32)
        else:
            source, local = None, block - 2
            shift = jnp.full((1, 128), shift_ref[local], jnp.int32)
        for h in range(HA):
            if source is None:
                biases.append(bias_ref[h, 32 * local : 32 * local + 32])
            else:
                at = 128 + HALF * h + 32 * local
                biases.append(source[at : at + 32])
        shifts.append(shift)
    for block, shift in zip(order, shifts):
        pick = jnp.where(offset == shift[:, 0:1], 1.0, 0.0).astype(BF16)
        windows.append(dot(pick, project[32 * block : 32 * block + 160, 128:]).astype(BF16))
        query = project[64 + 32 * block : 96 + 32 * block, :128].astype(F32)
        stacks.append(
            jnp.concatenate([query * head_mask[h] for h in range(HA)], axis=0).astype(BF16)
        )
    scores = [
        dot(stack, window[:, :128], NT) * (1.0 / math.sqrt(32))
        for stack, window in zip(stacks, windows)
    ]
    weights = []
    for n, block in enumerate(order):
        score = scores[n] + jnp.concatenate(biases[HA * n : HA * n + HA], axis=0).astype(F32)
        position = slot + (first + 32 * block - 112) + shifts[n]
        inside = (position >= 0) & (position < atom_count)
        score = jnp.where(inside, score, LOWEST)
        raised = jnp.exp(score - jnp.max(score, axis=-1, keepdims=True))
        weights.append((raised / jnp.sum(raised, axis=-1, keepdims=True)).astype(BF16))
    mixes = []
    for weight, window in zip(weights, windows):
        mixed = dot(weight, window[:, 128:])
        mix = mixed[0:32] * head_mask[0]
        for h in range(1, HA):
            mix = mix + mixed[32 * h : 32 * h + 32] * head_mask[h]
        mixes.append(mix)
    mixture = jnp.concatenate(mixes, axis=0).astype(BF16)
    base = jnp.concatenate([wide[128:320], wide[64:128]], axis=0)
    hidden = (base + dot(mixture, w_out_ref[...])).astype(BF16)
    hidden_ref[0:128] = hidden[:128]
    relative = (token_ref[...] - (16 * device - 16)).astype(F32)
    hidden_ref[128:144] = jnp.broadcast_to(relative, (16, 128)).astype(BF16)
    lifted = jnp.maximum(dot(hidden, w_pool_ref[...]), 0.0)
    own_token = (token_ref[...] - 16 * device).astype(F32)
    prev_token = prev_ref[448:449].astype(F32) - 33.0
    next_token = next_ref[448:449].astype(F32) - 1.0
    beside = jnp.where(iota((1, 128), 1) < HALF, next_token, prev_token)
    token = jnp.concatenate([own_token, beside], axis=1)
    select = jnp.where(iota((16, 256), 0).astype(F32) == token, 1.0, 0.0).astype(BF16)
    high, low = split(lifted)
    line = iota((16, 128), 0)
    count = jnp.zeros((16, 128), jnp.int32)
    live = jnp.zeros((16, 128), jnp.int32)
    for t in range(16):
        count = jnp.where(line == t, count_ref[t], count)
        live = jnp.where(line == t, mask_ref[t], live)
    count = jnp.concatenate([count.astype(F32)] * 6, axis=1)
    pooled = (dot(select, high) + dot(select, low)) / count
    pooled_ref[...] = pooled
    normed = normal(pooled).astype(BF16)
    cot = jnp.concatenate([cot_ref[...], next_ref[384:448], prev_ref[384:448]], axis=0)
    grad_up = dot(select, cot).astype(BF16)
    live = jnp.concatenate([live] * 6, axis=1)
    marked = jnp.where(live > 0, normed.astype(F32), MASKED).astype(BF16)
    for r in range(to_row_ref.shape[0]):
        to_row_ref[r] = marked
    to_col_ref[:, :768] = normed
    to_col_ref[:, 768:] = grad_up
    for copy in copies:
        copy.wait()


def window_of(head):
    block, rest = divmod(head, 8)
    return 384 * block + (0 if rest < 5 else 128)


def stack_kernel(own_ref, partner_ref, out_ref):
    row, col = place()
    core = lax.rem(col, 2)
    out_ref[core] = own_ref[...]
    out_ref[1 - core] = partner_ref[...]


def token_kernel(
    keys_ref,
    own_ref,
    first_ref,
    second_ref,
    third_ref,
    early_ref,
    late_ref,
    w_kv_ref,
    w_qkv_ref,
    w_out_ref,
    w_back_ref,
    pooled_ref,
    prob_ref,
    grad_ref,
    stats_ref,
    keep_ref,
    give_ref,
    pooled_out_ref,
    inner_out_ref,
    inner_back_ref,
    rows_ref,
    mixed_ref,
    inner_ref,
    bias_ref,
    arrived,
):
    copies = []
    for n in range(2):
        rows = slice(384 * n, 384 * (n + 1))
        copies.append((w_qkv_ref.at[rows, 0:768], inner_ref.at[rows]))
    copies.append((w_back_ref, inner_back_ref))
    for n in range(2):
        rows = slice(384 * n, 384 * (n + 1))
        copies.append((w_out_ref.at[rows], inner_out_ref.at[rows]))
    early = early_ref.shape[0]
    for first, count, source in ((0, early, early_ref), (early, 16 - early, late_ref)):
        for start, stop in ((0, count // 2), (count // 2, count)):
            copies.append(
                (source.at[start:stop], bias_ref.at[first + start : first + stop])
            )
    copies.append((pooled_ref, pooled_out_ref))
    copies = [pltpu.make_async_copy(a, b, arrived.at[n]) for n, (a, b) in enumerate(copies)]
    for copy in copies:
        copy.start()

    row, col = place()
    chip, core = lax.div(col, 2), lax.rem(col, 2)
    for s, part_ref in enumerate((own_ref, first_ref, second_ref, third_ref)):
        there = lax.rem(chip + 4 - s, 4) * 32
        rows_ref[pl.ds(pl.multiple_of(there, 32), 16)] = part_ref[0]
        rows_ref[pl.ds(pl.multiple_of(there + 16, 16), 16)] = part_ref[1]
    key = dot(keys_ref[...], w_kv_ref[:, :768]).astype(BF16)
    value = dot(keys_ref[...], w_kv_ref[:, 768:]).astype(BF16)
    for copy in copies[:2]:
        copy.wait()
    query = dot(rows_ref[:, :768], inner_ref[...]).astype(BF16)
    for copy in copies[2:5]:
        copy.wait()
    middle = dot(rows_ref[:, 768:], inner_back_ref[...], NT).astype(BF16)
    grad = dot(middle, inner_out_ref[...], NT).astype(BF16)
    first = keys_ref[:, :128].astype(F32).T[0:1]
    closed = jnp.where(first < MASKED, 0.0, -jnp.inf)
    lane = iota((128, 256), 1)
    stat_lane = iota((128, 128), 1)

    def within(h):
        at = window_of(h)
        return (lane >= 48 * h - at) & (lane < 48 * (h + 1) - at)

    for h in range(HT):
        at = window_of(h)
        grad_h = jnp.where(within(h), grad[:, at : at + 256].astype(F32), 0.0).astype(BF16)
        grads = dot(grad_h, value[:, at : at + 256], NT)
        grad_ref[:, h] = grads.reshape(16, GROUP, 256)
    for copy in copies[5:]:
        copy.wait()
    for h in range(HT):
        at = window_of(h)
        query_h = jnp.where(within(h), query[:, at : at + 256].astype(F32), 0.0).astype(BF16)
        scores = dot(query_h, key[:, at : at + 256], NT) * (1.0 / math.sqrt(48))
        bias = bias_ref[:, h].reshape(128, 256)
        prob_ref[:, h] = (scores + bias + closed).reshape(16, GROUP, 256)
    tops = jnp.zeros((128, 128), F32)
    sums = jnp.zeros((128, 128), F32)
    diags = jnp.zeros((128, 128), F32)
    for h in range(HT):
        scores = prob_ref[:, h].reshape(128, 256)
        top = jnp.maximum(jnp.max(scores, axis=-1, keepdims=True), LOWEST)
        high = top.astype(BF16).astype(F32)
        top = high + (top - high).astype(BF16).astype(F32)
        raised = jnp.exp(scores - top)
        prob_ref[:, h] = raised.reshape(16, GROUP, 256)
        total = jnp.sum(raised, axis=-1, keepdims=True)
        diag = jnp.sum(raised * grad_ref[:, h].reshape(128, 256), axis=-1, keepdims=True)
        here = stat_lane == h
        tops = jnp.where(here, top, tops)
        sums = jnp.where(here, total, sums)
        diags = jnp.where(here, diag, diags)
    for at in (0, 128, 384, 512):
        out = None
        for h in range(HT):
            if window_of(h) == at:
                raised = prob_ref[:, h].reshape(128, 256).astype(BF16)
                part = jnp.where(within(h), dot(raised, value[:, at : at + 256]), 0.0)
                out = part if out is None else out + part
        if at % 384 == 0:
            mixed_ref[:, at : at + 256] = out
        else:
            mixed_ref[:, at : at + 128] = mixed_ref[:, at : at + 128] + out[:, :128]
            mixed_ref[:, at + 128 : at + 256] = out[:, 128:]
    stats_ref[...] = tops + pltpu.roll(sums, 32, axis=1) + pltpu.roll(diags, 64, axis=1)
    packed = packed_stats(tops, sums, diags)
    for n in range(4):
        there = 32 * n + 16 * core
        keep_ref[n] = mixed_ref[pl.ds(pl.multiple_of(there, 16), 16)]
        there = 32 * n + 16 - 16 * core
        part = mixed_ref[pl.ds(pl.multiple_of(there, 16), 16)]
        give_ref[n, :, :768] = part.astype(BF16)
        for k in range(2):
            at = 32 * n + 16 * k
            give_ref[n, :, 768 + 128 * k : 896 + 128 * k] = packed[at : at + 16]


def packed_stats(tops, sums, diags):
    stats = jnp.zeros((128, 128), F32)
    for k, part in enumerate((tops, sums, diags)):
        high = part.astype(BF16).astype(F32)
        for n, piece in enumerate((high, part - high)):
            turn = 32 * k + 16 * n
            stats = stats + (pltpu.roll(piece, turn, axis=1) if turn else piece)
    return stats.astype(BF16)


def spread_heads(factors):
    spread = jnp.where(iota((128, 768), 1) // 48 == iota((128, 768), 0), 1.0, 0.0).astype(BF16)
    high, low = split(factors)
    return dot(high, spread) + dot(low, spread)


def parted_stats(stats):
    lane = iota((128, 128), 1)
    parts = [stats, pltpu.roll(stats, 96, axis=1), pltpu.roll(stats, 64, axis=1)]
    return [jnp.where(lane < HT, part, 0.0) for part in parts]


def fold_kernel(
    keep_ref,
    stats_ref,
    given_ref,
    first_ref,
    second_ref,
    third_ref,
    own_ref,
    joint_ref,
    ratio_ref,
    mixed_ref,
):
    row, col = place()
    chip, core = lax.div(col, 2), lax.rem(col, 2)
    given = jnp.concatenate(
        [given_ref[n, :, 768 + 128 * k : 896 + 128 * k] for n in range(4) for k in range(2)],
        axis=0,
    ).astype(F32)
    given = given + pltpu.roll(given, 112, axis=1)
    sides = [parted_stats(stats_ref[...]), parted_stats(given)]
    top = jnp.maximum(sides[0][0], sides[1][0])
    ratios = [jnp.exp(side[0] - top) for side in sides]
    total = ratios[0] * sides[0][1] + ratios[1] * sides[1][1]
    diag = ratios[0] * sides[0][2] + ratios[1] * sides[1][2]
    joint_ref[...] = top + pltpu.roll(total, 32, axis=1) + pltpu.roll(diag, 64, axis=1)
    ratio_ref[0] = ratios[0]
    ratio_ref[1] = ratios[1]
    rows = [pl.ds(pl.multiple_of(32 * n + 16 * core, 16), 16) for n in range(4)]
    factors = spread_heads(
        jnp.concatenate([ratio_ref[side, rows[n]] for side in range(2) for n in range(4)], axis=0)
    )
    for n in range(4):
        given_n = given_ref[n, :, :768].astype(F32)
        mixed_ref[n] = (
            keep_ref[n] * factors[16 * n : 16 * n + 16]
            + given_n * factors[64 + 16 * n : 80 + 16 * n]
        )
    packed = packed_stats(top, total, diag)
    for s, out_ref in enumerate((first_ref, second_ref, third_ref)):
        out_ref[:, :768] = mixed_ref[lax.rem(chip + s + 1, 4)].astype(BF16)
        for k in range(8):
            out_ref[:, 768 + 128 * k : 896 + 128 * k] = packed[16 * k : 16 * k + 16]
    own_ref[...] = mixed_ref[chip]


def merge_kernel(
    stats_ref,
    own_ref,
    joint_ref,
    first_ref,
    second_ref,
    third_ref,
    pooled_ref,
    w_out_ref,
    w_back_ref,
    scale_ref,
    diag_ref,
    low_ref,
    near_ref,
    far_ref,
    ratio_ref,
):
    row, col = place()
    lane = iota((128, 128), 1)
    sides = [parted_stats(joint_ref[...])]
    for part_ref in (first_ref, second_ref, third_ref):
        stats = jnp.concatenate(
            [part_ref[:, 768 + 128 * k : 896 + 128 * k] for k in range(8)], axis=0
        ).astype(F32)
        sides.append(parted_stats(stats + pltpu.roll(stats, 112, axis=1)))
    top = functools.reduce(jnp.maximum, [side[0] for side in sides])
    ratios = [jnp.exp(side[0] - top) for side in sides]
    total = functools.reduce(jnp.add, [r * side[1] for r, side in zip(ratios, sides)])
    diag = functools.reduce(jnp.add, [r * side[2] for r, side in zip(ratios, sides)])
    inverse = 1.0 / jnp.where(lane < HT, total, 1.0)
    for n in range(4):
        ratio_ref[n] = ratios[n] * inverse
    own_top = parted_stats(stats_ref[...])[0]
    scale_ref[...] = jnp.exp(own_top - top) * inverse
    diag_ref[...] = diag * inverse
    rows = pl.ds(pl.multiple_of(col * 16, 16), 16)
    factors = spread_heads(jnp.concatenate([ratio_ref[n, rows] for n in range(4)], axis=0))
    mixed = own_ref[...] * factors[0:16]
    for n, part_ref in enumerate((first_ref, second_ref, third_ref)):
        mixed = mixed + part_ref[:, :768].astype(F32) * factors[16 * n + 16 : 16 * n + 32]
    updated = (pooled_ref[...] + dot(mixed.astype(BF16), w_out_ref[...])).astype(BF16)
    high, low = split(dot(updated, w_back_ref[...]))
    near_ref[...] = high
    far_ref[...] = high
    low_ref[0] = high
    low_ref[1] = low


def pair_grad_kernel(prob_ref, grad_ref, scale_ref, diag_ref, head_ref, out_ref, tile_ref, left):
    groups = prob_ref.shape[0]

    def copy(g):
        rows = pl.ds(g * GROUP, GROUP)
        return pltpu.make_async_copy(tile_ref.at[rows], out_ref.at[rows], left.at[g])

    head_rows = head_ref[...].astype(F32)
    weights = jnp.concatenate([grouped_weight(head_rows, i) for i in range(GROUP)], axis=1)

    def score_of(g):
        rows = pl.ds(pl.multiple_of(g * GROUP, GROUP), GROUP)
        scale = scale_ref[rows]
        diag = diag_ref[rows]
        score = jnp.concatenate(
            [
                prob_ref[g, h] * scale[:, h : h + 1] * (grad_ref[g, h] - diag[:, h : h + 1])
                for h in range(HT)
            ],
            axis=0,
        )
        return score.T.astype(BF16)

    def step(g, score):
        following = score_of(jnp.minimum(g + 1, groups - 1))
        result = dot(score, weights)
        for i in range(GROUP):
            tile_ref[g * GROUP + i] = result[:, 128 * i : 128 * (i + 1)].astype(BF16)
        copy(g).start()
        return following

    lax.fori_loop(0, groups, step, score_of(0), unroll=2)
    for g in range(groups):
        copy(g).wait()


def atom_out_kernel(near_ref, far_ref, low_ref, hidden_ref, out_ref):
    row, col = place()
    odd = lax.rem(col, 2) == 1
    near = near_ref[...].astype(F32)
    far = far_ref[...].astype(F32)
    before = jnp.where(odd, near, far).astype(BF16)
    after = jnp.where(odd, far, near).astype(BF16)
    rows = jnp.concatenate([before, low_ref[0], after, low_ref[1]], axis=0)
    token = hidden_ref[128:144].astype(F32)[0:1]
    index = iota((64, 128), 0)
    index = jnp.where(index < 48, index, index - 32).astype(F32)
    select = jnp.where(index == token, 1.0, 0.0).astype(BF16)
    out_ref[...] = (hidden_ref[0:128].astype(F32) + dot(select, rows, TN)).astype(BF16)


def shards(
    atoms,
    atom_bias,
    key_shift,
    atom_token,
    token_atoms,
    token_mask,
    pair,
    w_atom_qkv,
    w_atom_out,
    w_pool,
    w_token_qkv,
    w_token_out,
    w_bias,
    w_back,
    cotangent,
):
    row_count, col_count = lax.axis_size("row"), lax.axis_size("col")
    devices = row_count * col_count
    core_pairs = [(i, i ^ 1) for i in range(col_count)]
    chip_pairs = [(i, i + 1) for i in range(1, devices - 1, 2)]
    chip_pairs = chip_pairs + [(j, i) for i, j in chip_pairs]

    def chip_shift(steps):
        return [(i, (i + 2 * steps) % col_count) for i in range(col_count)]

    tokens = atom_token.reshape(1, 128)
    payload = jax.ShapeDtypeStruct((464, 128), BF16)
    near, far = pl.pallas_call(
        pack_kernel,
        in_specs=[SMEM] + [VMEM] * 4,
        out_specs=[VMEM, VMEM],
        out_shape=[payload, payload],
        compiler_params=params(4),
        name="pack",
        cost_estimate=pl.CostEstimate(flops=0, bytes_accessed=1 << 20, transcendentals=0),
    )(
        outside(key_shift),
        outside(atoms),
        outside(atom_bias),
        outside(cotangent),
        outside(tokens),
    )
    near = lax.ppermute(near, "col", core_pairs)
    far = lax.ppermute(far, ("row", "col"), chip_pairs)

    tile = pair.reshape(128, 256, 128)
    head_rows = jnp.repeat(jnp.transpose(w_bias), GROUP, axis=0)
    def pair_bias(first, groups, name):
        return pl.pallas_call(
            functools.partial(pair_bias_kernel, first),
            in_specs=[HBM, VMEM],
            out_specs=HBM,
            out_shape=pltpu.HBM((groups, HT, GROUP, 256), F32),
            scratch_shapes=[
                pltpu.VMEM((groups * GROUP, 256, 128), BF16),
                pltpu.VMEM((groups, HT, GROUP, 256), F32),
                pltpu.SemaphoreType.DMA((groups,)),
                pltpu.SemaphoreType.DMA((groups,)),
            ],
            compiler_params=params(14),
            name=name,
            cost_estimate=pl.CostEstimate(
                flops=groups << 26, bytes_accessed=groups << 19, transcendentals=0
            ),
        )(outside(tile), head_rows)

    half = EARLY
    early = pair_bias(0, half, "pair_bias_early")
    late = pair_bias(half, 16 - half, "pair_bias_late")

    hidden, pooled, to_row, to_col, token_kv = pl.pallas_call(
        atom_kernel,
        in_specs=[SMEM] * 3 + [VMEM] * 6 + [pl.BlockSpec(memory_space=pl.ANY)] + [VMEM] * 3 + [HBM],
        out_specs=[VMEM] * 5,
        out_shape=[
            pltpu.VMEM((144, 128), BF16),
            pltpu.HBM((16, 768), F32),
            pltpu.VMEM((row_count, 16, 768), BF16),
            pltpu.VMEM((16, 896), BF16),
            pltpu.VMEM((768, 1536), BF16),
        ],
        scratch_shapes=[
            pltpu.VMEM((464, 128), BF16),
            pltpu.VMEM((464, 128), BF16),
            pltpu.SemaphoreType.DMA((4,)),
        ],
        compiler_params=params(8),
        name="atom_stage",
        cost_estimate=pl.CostEstimate(flops=1 << 28, bytes_accessed=2 << 20, transcendentals=1 << 17),
    )(
        outside(key_shift),
        outside(token_atoms),
        outside(token_mask),
        near,
        far,
        outside(atoms),
        outside(atom_bias),
        outside(cotangent),
        outside(tokens),
        outside(early),
        outside(w_atom_qkv),
        outside(w_atom_out),
        outside(w_pool),
        outside(w_token_qkv),
    )
    partner = lax.ppermute(to_col, "col", core_pairs)
    keys = lax.all_to_all(to_row, "row", 0, 0).reshape(256, 768)
    own = pl.pallas_call(
        stack_kernel,
        in_specs=[VMEM] * 2,
        out_specs=VMEM,
        out_shape=pltpu.VMEM((2, 16, 896), BF16),
        compiler_params=params(4),
        name="stack",
        cost_estimate=pl.CostEstimate(flops=1 << 32, bytes_accessed=1 << 18, transcendentals=0),
    )(inside(to_col), partner)
    shifted = [lax.ppermute(own, "col", chip_shift(s)) for s in range(1, 4)]

    stat = pltpu.VMEM((128, 128), F32)
    swapped = jax.ShapeDtypeStruct((4, 16, 1024), BF16)
    folded = jax.ShapeDtypeStruct((16, 1792), BF16)
    table = pltpu.VMEM((16, HT, GROUP, 256), F32)
    prob, grad, stats, keep, give, pooled, token_out, back = pl.pallas_call(
        token_kernel,
        in_specs=[VMEM] * 5 + [HBM] * 2 + [VMEM] + [HBM] * 4,
        out_specs=[VMEM] * 8,
        scratch_shapes=[
            pltpu.VMEM((128, 896), BF16),
            pltpu.VMEM((128, 768), F32),
            pltpu.VMEM((768, 768), BF16),
            pltpu.VMEM((16, HT, GROUP, 256), F32),
            pltpu.SemaphoreType.DMA((10,)),
        ],
        out_shape=[
            table,
            table,
            stat,
            pltpu.VMEM((4, 16, 768), F32),
            swapped,
            pltpu.VMEM((16, 768), F32),
            pltpu.VMEM(w_token_out.shape, BF16),
            pltpu.VMEM(w_back.shape, BF16),
        ],
        compiler_params=params(16),
        name="token_stage",
        cost_estimate=pl.CostEstimate(flops=1 << 31, bytes_accessed=12 << 20, transcendentals=1 << 19),
    )(
        inside(keys),
        inside(own),
        *shifted,
        outside(early),
        outside(late),
        inside(token_kv),
        outside(w_token_qkv),
        outside(w_token_out),
        outside(w_back),
        outside(pooled),
    )
    given = lax.ppermute(give, "col", core_pairs)
    *sent, mixed, joint = pl.pallas_call(
        fold_kernel,
        in_specs=[VMEM] * 3,
        out_specs=[VMEM] * 5,
        out_shape=[folded, folded, folded, pltpu.VMEM((16, 768), F32), stat],
        scratch_shapes=[pltpu.VMEM((2, 128, 128), F32), pltpu.VMEM((4, 16, 768), F32)],
        compiler_params=params(6),
        name="fold",
        cost_estimate=pl.CostEstimate(flops=1 << 26, bytes_accessed=2 << 20, transcendentals=1 << 17),
    )(inside(keep), inside(stats), given)
    parts = [lax.ppermute(part, "col", chip_shift(s + 1)) for s, part in enumerate(sent)]

    scale, diag, low, near, far = pl.pallas_call(
        merge_kernel,
        in_specs=[VMEM] * 9,
        out_specs=[VMEM] * 5,
        out_shape=[
            stat,
            stat,
            pltpu.VMEM((2, 16, 128), BF16),
            jax.ShapeDtypeStruct((16, 128), BF16),
            jax.ShapeDtypeStruct((16, 128), BF16),
        ],
        scratch_shapes=[pltpu.VMEM((4, 128, 128), F32)],
        compiler_params=params(6),
        name="merge",
        cost_estimate=pl.CostEstimate(flops=1 << 26, bytes_accessed=2 << 20, transcendentals=1 << 17),
    )(
        inside(stats),
        inside(mixed),
        inside(joint),
        *parts,
        inside(pooled),
        inside(token_out),
        inside(back),
    )
    near = lax.ppermute(near, "col", core_pairs)
    far = lax.ppermute(far, ("row", "col"), chip_pairs)

    pair_grad = pl.pallas_call(
        pair_grad_kernel,
        in_specs=[VMEM] * 5,
        out_specs=HBM,
        out_shape=jax.ShapeDtypeStruct((128, 256, 128), BF16),
        scratch_shapes=[pltpu.VMEM((128, 256, 128), BF16), pltpu.SemaphoreType.DMA((16,))],
        compiler_params=params(14),
        name="pair_grad",
        cost_estimate=pl.CostEstimate(
            flops=2 * 128 * 256 * 128 * 16 * 8, bytes_accessed=14 << 20, transcendentals=0
        ),
    )(inside(prob), inside(grad), inside(scale), inside(diag), head_rows)
    atom_out = pl.pallas_call(
        atom_out_kernel,
        in_specs=[VMEM] * 4,
        out_specs=VMEM,
        out_shape=jax.ShapeDtypeStruct((128, 128), BF16),
        compiler_params=params(4),
        name="atom_out",
        cost_estimate=pl.CostEstimate(flops=1 << 21, bytes_accessed=1 << 17, transcendentals=0),
    )(near, far, inside(low), inside(hidden))
    return (atom_out, pair_grad.reshape(pair.shape))


def solution(mesh):
    return jax.shard_map(
        shards,
        mesh=mesh,
        in_specs=(
            P(("row", "col"), None),
            P(None, ("row", "col"), None),
            P(("row", "col")),
            P(("row", "col")),
            P(("row", "col")),
            P(("row", "col")),
            P("row", None, "col", None, None),
            P(),
            P(),
            P(),
            P(),
            P(),
            P(),
            P(),
            P(("row", "col"), None),
        ),
        out_specs=(P(("row", "col"), None), P("row", None, "col", None, None)),
        check_vma=False,
    )
```

```python
import functools
import math

import jax
import jax.numpy as jnp
from jax import lax
from jax.experimental import pallas as pl
from jax.experimental.pallas import tpu as pltpu
from jax.sharding import PartitionSpec as P

HA = 4
HT = 16
QB = 32
KW = 128
SHIFT = 16
HALF = 64
EARLY = 8
GROUP = 8
AUX = 16
EPSILON = 1e-05
LOWEST = -1e30
MASKED = 1024.0
F32 = jnp.float32
BF16 = jnp.bfloat16
NT = (((1,), (1,)), ((), ()))
TN = (((0,), (0,)), ((), ()))

VMEM = pl.BlockSpec(memory_space=pltpu.VMEM)
HBM = pl.BlockSpec(memory_space=pltpu.HBM)
SMEM = pl.BlockSpec(memory_space=pltpu.SMEM)


def params(mib):
    return pltpu.CompilerParams(vmem_limit_bytes=mib << 20)


def outside(value):
    return pltpu.with_memory_space_constraint(value, pltpu.HBM)


def inside(value):
    return pltpu.with_memory_space_constraint(value, pltpu.VMEM)


def place():
    return lax.axis_index("row"), lax.axis_index("col")


def iota(shape, dim):
    return lax.broadcasted_iota(jnp.int32, shape, dim)


def dot(a, b, dims=None):
    if dims is None:
        return jnp.dot(a, b, preferred_element_type=F32)
    return lax.dot_general(a, b, dims, preferred_element_type=F32)


def normal(values):
    centred = values - jnp.mean(values, axis=-1, keepdims=True)
    return centred * lax.rsqrt(jnp.mean(centred * centred, axis=-1, keepdims=True) + EPSILON)


def split(values):
    high = values.astype(BF16)
    return high, (values - high.astype(F32)).astype(BF16)


def grouped_weight(head_rows, member):
    rows = iota(head_rows.shape, 0)
    return jnp.where(rows % GROUP == member, head_rows, 0.0).astype(BF16)


def pair_bias_kernel(first, pair_ref, head_ref, *refs):
    *brought, tile_ref, bias_ref, arrived, left, came = refs
    extra = len(brought) // 2
    out_ref = brought[extra]
    extras = [
        pltpu.make_async_copy(brought[n], brought[extra + 1 + n], came.at[n]) for n in range(extra)
    ]
    groups = out_ref.shape[0]
    window = min(8, groups)

    def copy(g):
        rows = pl.ds(g * GROUP, GROUP)
        here = pl.ds((g + first) * GROUP, GROUP)
        return pltpu.make_async_copy(pair_ref.at[here], tile_ref.at[rows], arrived.at[g])

    def leave(g):
        return pltpu.make_async_copy(bias_ref.at[g], out_ref.at[g], left.at[g])

    for g in range(window):
        copy(g).start()
    for extra_copy in extras:
        extra_copy.start()
    weight = head_ref[...].astype(F32).reshape(HT, GROUP, 128)[:, 0].astype(BF16)

    def step(g, carry):
        copy(g).wait()
        if window < groups:

            @pl.when(g + window < groups)
            def _():
                copy(g + window).start()

        for i in range(GROUP):
            bias_ref[g, :, i, :] = dot(weight, tile_ref[g * GROUP + i], NT)
        leave(g).start()
        return carry

    lax.fori_loop(0, groups, step, 0, unroll=groups)
    for g in range(groups):
        leave(g).wait()
    for extra_copy in extras:
        extra_copy.wait()


def pack_kernel(
    shift_ref,
    count_ref,
    mask_ref,
    atoms_ref,
    bias_ref,
    cot_ref,
    token_ref,
    near_ref,
    far_ref,
    side_ref,
):
    row, col = place()
    odd = lax.rem(col, 2)
    line = iota((AUX, 128), 0)
    device = row * lax.axis_size("col") + col
    aux = jnp.where(line == 0, token_ref[...] - (16 * device - 17), 0)
    for n in range(4):
        aux = jnp.where(line == 1 + n, shift_ref[n], aux)
    wide = aux.astype(F32)
    aux = wide.astype(BF16)

    def fill(out_ref, at):
        out_ref[0:128] = atoms_ref[...]
        for h in range(HA):
            out_ref[128 + HALF * h : 128 + HALF * (h + 1)] = bias_ref[h, at : at + HALF]
        out_ref[384:448] = cot_ref[at : at + HALF]
        out_ref[448:464] = aux

    side_ref[0:16] = wide
    count = jnp.zeros((16, 128), jnp.int32)
    live = jnp.zeros((16, 128), jnp.int32)
    for t in range(16):
        count = jnp.where(line == t, count_ref[t], count)
        live = jnp.where(line == t, mask_ref[t], live)
    side_ref[16:32] = count.astype(F32)
    side_ref[32:48] = live.astype(F32)

    @pl.when(odd == 1)
    def _():
        fill(near_ref, 0)
        fill(far_ref, HALF)

    @pl.when(odd == 0)
    def _():
        fill(near_ref, HALF)
        fill(far_ref, 0)


def atom_kernel(
    side_ref,
    near_ref,
    far_ref,
    atoms_ref,
    bias_ref,
    cot_ref,
    w_qkv_ref,
    w_out_ref,
    w_pool_ref,
    token_qkv_ref,
    hidden_ref,
    pooled_ref,
    to_row_ref,
    to_col_ref,
    token_kv_ref,
    prev_ref,
    next_ref,
    arrived,
):
    copies = []
    for n in range(4):
        rows = slice(192 * n, 192 * (n + 1))
        copies.append(
            pltpu.make_async_copy(
                token_qkv_ref.at[rows, 768:2304], token_kv_ref.at[rows], arrived.at[n]
            )
        )
    for copy in copies:
        copy.start()
    row, col = place()
    odd = lax.rem(col, 2)
    device = row * lax.axis_size("col") + col
    atom_count = 128 * lax.axis_size("row") * lax.axis_size("col")

    @pl.when(odd == 1)
    def _():
        prev_ref[...] = near_ref[...]
        next_ref[...] = far_ref[...]

    @pl.when(odd == 0)
    def _():
        prev_ref[...] = far_ref[...]
        next_ref[...] = near_ref[...]

    first = device * 128
    extended = jnp.concatenate([prev_ref[0:128], atoms_ref[...], next_ref[0:128]], axis=0)
    wide = extended.astype(F32)
    project = dot(normal(wide).astype(BF16), w_qkv_ref[...]).astype(BF16)
    head_lane = iota((QB, 128), 1) // 32
    head_mask = [jnp.where(head_lane == h, 1.0, 0.0) for h in range(HA)]
    slot = iota((1, KW), 1)
    offset = iota((KW, 160), 1) - iota((KW, 160), 0) - SHIFT
    order = (2, 3, 4, 5, 6, 7, 0, 1)
    biases, shifts, windows, stacks = [], [], [], []
    for block in order:
        if block < 2:
            source, local = prev_ref, block
            shift = prev_ref[451 + local : 452 + local].astype(F32).astype(jnp.int32)
        elif block > 5:
            source, local = next_ref, block - 6
            shift = next_ref[449 + local : 450 + local].astype(F32).astype(jnp.int32)
        else:
            source, local = None, block - 2
            shift = side_ref[1 + local : 2 + local].astype(jnp.int32)
        for h in range(HA):
            if source is None:
                biases.append(bias_ref[h, 32 * local : 32 * local + 32])
            else:
                at = 128 + HALF * h + 32 * local
                biases.append(source[at : at + 32])
        shifts.append(shift)
    for block, shift in zip(order, shifts):
        pick = jnp.where(offset == shift[:, 0:1], 1.0, 0.0).astype(BF16)
        windows.append(dot(pick, project[32 * block : 32 * block + 160, 128:]).astype(BF16))
        query = project[64 + 32 * block : 96 + 32 * block, :128].astype(F32)
        stacks.append(
            jnp.concatenate([query * head_mask[h] for h in range(HA)], axis=0).astype(BF16)
        )
    scores = [
        dot(stack, window[:, :128], NT) * (1.0 / math.sqrt(32))
        for stack, window in zip(stacks, windows)
    ]
    weights = []
    for n, block in enumerate(order):
        score = scores[n] + jnp.concatenate(biases[HA * n : HA * n + HA], axis=0).astype(F32)
        position = slot + (first + 32 * block - 112) + shifts[n]
        inside = (position >= 0) & (position < atom_count)
        score = jnp.where(inside, score, LOWEST)
        raised = jnp.exp(score - jnp.max(score, axis=-1, keepdims=True))
        weights.append((raised / jnp.sum(raised, axis=-1, keepdims=True)).astype(BF16))
    mixes = []
    for weight, window in zip(weights, windows):
        mixed = dot(weight, window[:, 128:])
        mix = mixed[0:32] * head_mask[0]
        for h in range(1, HA):
            mix = mix + mixed[32 * h : 32 * h + 32] * head_mask[h]
        mixes.append(mix)
    mixture = jnp.concatenate(mixes, axis=0).astype(BF16)
    base = jnp.concatenate([wide[128:320], wide[64:128]], axis=0)
    hidden = (base + dot(mixture, w_out_ref[...])).astype(BF16)
    hidden_ref[0:128] = hidden[:128]
    relative = side_ref[0:1] - 1.0
    hidden_ref[128:144] = jnp.broadcast_to(relative, (16, 128)).astype(BF16)
    lifted = jnp.maximum(dot(hidden, w_pool_ref[...]), 0.0)
    own_token = side_ref[0:1] - 17.0
    prev_token = prev_ref[448:449].astype(F32) - 33.0
    next_token = next_ref[448:449].astype(F32) - 1.0
    beside = jnp.where(iota((1, 128), 1) < HALF, next_token, prev_token)
    token = jnp.concatenate([own_token, beside], axis=1)
    select = jnp.where(iota((16, 256), 0).astype(F32) == token, 1.0, 0.0).astype(BF16)
    high, low = split(lifted)
    count = jnp.concatenate([side_ref[16:32]] * 6, axis=1)
    pooled = (dot(select, high) + dot(select, low)) / count
    pooled_ref[...] = pooled
    normed = normal(pooled).astype(BF16)
    cot = jnp.concatenate([cot_ref[...], next_ref[384:448], prev_ref[384:448]], axis=0)
    grad_up = dot(select, cot).astype(BF16)
    live = jnp.concatenate([side_ref[32:48]] * 6, axis=1)
    marked = jnp.where(live > 0, normed.astype(F32), MASKED).astype(BF16)
    for r in range(to_row_ref.shape[0]):
        to_row_ref[r] = marked
    to_col_ref[:, :768] = normed
    to_col_ref[:, 768:] = grad_up
    for copy in copies:
        copy.wait()


def window_of(head):
    block, rest = divmod(head, 8)
    return 384 * block + (0 if rest < 5 else 128)


def stack_kernel(own_ref, partner_ref, out_ref):
    row, col = place()
    core = lax.rem(col, 2)
    out_ref[core] = own_ref[...]
    out_ref[1 - core] = partner_ref[...]


def token_kernel(
    keys_ref,
    own_ref,
    first_ref,
    second_ref,
    third_ref,
    early_ref,
    late_ref,
    w_kv_ref,
    w_qkv_ref,
    w_out_ref,
    w_back_ref,
    pooled_ref,
    prob_ref,
    grad_ref,
    stats_ref,
    keep_ref,
    give_ref,
    pooled_out_ref,
    inner_out_ref,
    inner_back_ref,
    rows_ref,
    mixed_ref,
    inner_ref,
    bias_ref,
    arrived,
):
    copies = []
    for n in range(2):
        rows = slice(384 * n, 384 * (n + 1))
        copies.append((w_qkv_ref.at[rows, 0:768], inner_ref.at[rows]))
    copies.append((w_back_ref, inner_back_ref))
    for n in range(2):
        rows = slice(384 * n, 384 * (n + 1))
        copies.append((w_out_ref.at[rows], inner_out_ref.at[rows]))
    early = early_ref.shape[0]
    for first, count, source in ((0, early, early_ref), (early, 16 - early, late_ref)):
        for start, stop in ((0, count // 2), (count // 2, count)):
            copies.append(
                (source.at[start:stop], bias_ref.at[first + start : first + stop])
            )
    copies.append((pooled_ref, pooled_out_ref))
    copies = [pltpu.make_async_copy(a, b, arrived.at[n]) for n, (a, b) in enumerate(copies)]
    for copy in copies[:5]:
        copy.start()

    row, col = place()
    chip, core = lax.div(col, 2), lax.rem(col, 2)
    for s, part_ref in enumerate((own_ref, first_ref, second_ref, third_ref)):
        there = lax.rem(chip + 4 - s, 4) * 32
        rows_ref[pl.ds(pl.multiple_of(there, 32), 16)] = part_ref[0]
        rows_ref[pl.ds(pl.multiple_of(there + 16, 16), 16)] = part_ref[1]
    key = dot(keys_ref[...], w_kv_ref[:, :768]).astype(BF16)
    value = dot(keys_ref[...], w_kv_ref[:, 768:]).astype(BF16)
    for copy in copies[5:]:
        copy.start()
    for copy in copies[:2]:
        copy.wait()
    query = dot(rows_ref[:, :768], inner_ref[...]).astype(BF16)
    for copy in copies[2:5]:
        copy.wait()
    middle = dot(rows_ref[:, 768:], inner_back_ref[...], NT).astype(BF16)
    grad = dot(middle, inner_out_ref[...], NT).astype(BF16)
    first = keys_ref[:, :128].astype(F32).T[0:1]
    closed = jnp.where(first < MASKED, 0.0, -jnp.inf)
    lane = iota((128, 256), 1)
    stat_lane = iota((128, 128), 1)

    def within(h):
        at = window_of(h)
        return (lane >= 48 * h - at) & (lane < 48 * (h + 1) - at)

    for h in range(HT):
        at = window_of(h)
        grad_h = jnp.where(within(h), grad[:, at : at + 256].astype(F32), 0.0).astype(BF16)
        grads = dot(grad_h, value[:, at : at + 256], NT)
        grad_ref[:, h] = grads.reshape(16, GROUP, 256)
    for copy in copies[5:]:
        copy.wait()
    for h in range(HT):
        at = window_of(h)
        query_h = jnp.where(within(h), query[:, at : at + 256].astype(F32), 0.0).astype(BF16)
        scores = dot(query_h, key[:, at : at + 256], NT) * (1.0 / math.sqrt(48))
        bias = bias_ref[:, h].reshape(128, 256)
        prob_ref[:, h] = (scores + bias + closed).reshape(16, GROUP, 256)
    tops = jnp.zeros((128, 128), F32)
    sums = jnp.zeros((128, 128), F32)
    diags = jnp.zeros((128, 128), F32)
    for h in range(HT):
        scores = prob_ref[:, h].reshape(128, 256)
        top = jnp.maximum(jnp.max(scores, axis=-1, keepdims=True), LOWEST)
        high = top.astype(BF16).astype(F32)
        top = high + (top - high).astype(BF16).astype(F32)
        raised = jnp.exp(scores - top)
        prob_ref[:, h] = raised.reshape(16, GROUP, 256)
        total = jnp.sum(raised, axis=-1, keepdims=True)
        diag = jnp.sum(raised * grad_ref[:, h].reshape(128, 256), axis=-1, keepdims=True)
        here = stat_lane == h
        tops = jnp.where(here, top, tops)
        sums = jnp.where(here, total, sums)
        diags = jnp.where(here, diag, diags)
    for at in (0, 128, 384, 512):
        out = None
        for h in range(HT):
            if window_of(h) == at:
                raised = prob_ref[:, h].reshape(128, 256).astype(BF16)
                part = jnp.where(within(h), dot(raised, value[:, at : at + 256]), 0.0)
                out = part if out is None else out + part
        if at % 384 == 0:
            mixed_ref[:, at : at + 256] = out
        else:
            mixed_ref[:, at : at + 128] = mixed_ref[:, at : at + 128] + out[:, :128]
            mixed_ref[:, at + 128 : at + 256] = out[:, 128:]
    stats_ref[...] = tops + pltpu.roll(sums, 32, axis=1) + pltpu.roll(diags, 64, axis=1)
    packed = packed_stats(tops, sums, diags)
    for n in range(4):
        there = 32 * n + 16 * core
        keep_ref[n] = mixed_ref[pl.ds(pl.multiple_of(there, 16), 16)]
        there = 32 * n + 16 - 16 * core
        part = mixed_ref[pl.ds(pl.multiple_of(there, 16), 16)]
        give_ref[n, :, :768] = part.astype(BF16)
        for k in range(2):
            at = 32 * n + 16 * k
            give_ref[n, :, 768 + 128 * k : 896 + 128 * k] = packed[at : at + 16]


def packed_stats(tops, sums, diags):
    stats = jnp.zeros((128, 128), F32)
    for k, part in enumerate((tops, sums, diags)):
        high = part.astype(BF16).astype(F32)
        for n, piece in enumerate((high, part - high)):
            turn = 32 * k + 16 * n
            stats = stats + (pltpu.roll(piece, turn, axis=1) if turn else piece)
    return stats.astype(BF16)


def spread_heads(factors):
    spread = jnp.where(iota((128, 768), 1) // 48 == iota((128, 768), 0), 1.0, 0.0).astype(BF16)
    high, low = split(factors)
    return dot(high, spread) + dot(low, spread)


def parted_stats(stats):
    lane = iota((128, 128), 1)
    parts = [stats, pltpu.roll(stats, 96, axis=1), pltpu.roll(stats, 64, axis=1)]
    return [jnp.where(lane < HT, part, 0.0) for part in parts]


def fold_kernel(
    keep_ref,
    stats_ref,
    given_ref,
    first_ref,
    second_ref,
    third_ref,
    own_ref,
    joint_ref,
    ratio_ref,
    mixed_ref,
):
    row, col = place()
    chip, core = lax.div(col, 2), lax.rem(col, 2)
    given = jnp.concatenate(
        [given_ref[n, :, 768 + 128 * k : 896 + 128 * k] for n in range(4) for k in range(2)],
        axis=0,
    ).astype(F32)
    given = given + pltpu.roll(given, 112, axis=1)
    sides = [parted_stats(stats_ref[...]), parted_stats(given)]
    top = jnp.maximum(sides[0][0], sides[1][0])
    ratios = [jnp.exp(side[0] - top) for side in sides]
    total = ratios[0] * sides[0][1] + ratios[1] * sides[1][1]
    diag = ratios[0] * sides[0][2] + ratios[1] * sides[1][2]
    joint_ref[...] = top + pltpu.roll(total, 32, axis=1) + pltpu.roll(diag, 64, axis=1)
    ratio_ref[0] = ratios[0]
    ratio_ref[1] = ratios[1]
    rows = [pl.ds(pl.multiple_of(32 * n + 16 * core, 16), 16) for n in range(4)]
    factors = spread_heads(
        jnp.concatenate([ratio_ref[side, rows[n]] for side in range(2) for n in range(4)], axis=0)
    )
    for n in range(4):
        given_n = given_ref[n, :, :768].astype(F32)
        mixed_ref[n] = (
            keep_ref[n] * factors[16 * n : 16 * n + 16]
            + given_n * factors[64 + 16 * n : 80 + 16 * n]
        )
    packed = packed_stats(top, total, diag)
    for s, out_ref in enumerate((first_ref, second_ref, third_ref)):
        out_ref[:, :768] = mixed_ref[lax.rem(chip + s + 1, 4)].astype(BF16)
        for k in range(8):
            out_ref[:, 768 + 128 * k : 896 + 128 * k] = packed[16 * k : 16 * k + 16]
    own_ref[...] = mixed_ref[chip]


def merge_kernel(
    stats_ref,
    own_ref,
    joint_ref,
    first_ref,
    second_ref,
    third_ref,
    pooled_ref,
    w_out_ref,
    w_back_ref,
    scale_ref,
    diag_ref,
    low_ref,
    near_ref,
    far_ref,
    ratio_ref,
):
    row, col = place()
    lane = iota((128, 128), 1)
    sides = [parted_stats(joint_ref[...])]
    for part_ref in (first_ref, second_ref, third_ref):
        stats = jnp.concatenate(
            [part_ref[:, 768 + 128 * k : 896 + 128 * k] for k in range(8)], axis=0
        ).astype(F32)
        sides.append(parted_stats(stats + pltpu.roll(stats, 112, axis=1)))
    top = functools.reduce(jnp.maximum, [side[0] for side in sides])
    ratios = [jnp.exp(side[0] - top) for side in sides]
    total = functools.reduce(jnp.add, [r * side[1] for r, side in zip(ratios, sides)])
    diag = functools.reduce(jnp.add, [r * side[2] for r, side in zip(ratios, sides)])
    inverse = 1.0 / jnp.where(lane < HT, total, 1.0)
    for n in range(4):
        ratio_ref[n] = ratios[n] * inverse
    own_top = parted_stats(stats_ref[...])[0]
    scale_ref[...] = jnp.exp(own_top - top) * inverse
    diag_ref[...] = diag * inverse
    rows = pl.ds(pl.multiple_of(col * 16, 16), 16)
    factors = spread_heads(jnp.concatenate([ratio_ref[n, rows] for n in range(4)], axis=0))
    mixed = own_ref[...] * factors[0:16]
    for n, part_ref in enumerate((first_ref, second_ref, third_ref)):
        mixed = mixed + part_ref[:, :768].astype(F32) * factors[16 * n + 16 : 16 * n + 32]
    updated = (pooled_ref[...] + dot(mixed.astype(BF16), w_out_ref[...])).astype(BF16)
    high, low = split(dot(updated, w_back_ref[...]))
    near_ref[...] = high
    far_ref[...] = high
    low_ref[0] = high
    low_ref[1] = low


def pair_grad_kernel(prob_ref, grad_ref, scale_ref, diag_ref, head_ref, out_ref, tile_ref, left):
    groups = prob_ref.shape[0]

    def copy(g):
        rows = pl.ds(g * GROUP, GROUP)
        return pltpu.make_async_copy(tile_ref.at[rows], out_ref.at[rows], left.at[g])

    head_rows = head_ref[...].astype(F32)
    weights = jnp.concatenate([grouped_weight(head_rows, i) for i in range(GROUP)], axis=1)

    def score_of(g):
        rows = pl.ds(pl.multiple_of(g * GROUP, GROUP), GROUP)
        scale = scale_ref[rows]
        diag = diag_ref[rows]
        score = jnp.concatenate(
            [
                prob_ref[g, h] * scale[:, h : h + 1] * (grad_ref[g, h] - diag[:, h : h + 1])
                for h in range(HT)
            ],
            axis=0,
        )
        return score.T.astype(BF16)

    def step(g, score):
        following = score_of(jnp.minimum(g + 1, groups - 1))
        result = dot(score, weights)
        for i in range(GROUP):
            tile_ref[g * GROUP + i] = result[:, 128 * i : 128 * (i + 1)].astype(BF16)
        copy(g).start()
        return following

    lax.fori_loop(0, groups, step, score_of(0), unroll=groups)
    for g in range(groups):
        copy(g).wait()


def atom_out_kernel(near_ref, far_ref, low_ref, hidden_ref, out_ref):
    row, col = place()
    odd = lax.rem(col, 2) == 1
    near = near_ref[...].astype(F32)
    far = far_ref[...].astype(F32)
    before = jnp.where(odd, near, far).astype(BF16)
    after = jnp.where(odd, far, near).astype(BF16)
    rows = jnp.concatenate([before, low_ref[0], after, low_ref[1]], axis=0)
    token = hidden_ref[128:144].astype(F32)[0:1]
    index = iota((64, 128), 0)
    index = jnp.where(index < 48, index, index - 32).astype(F32)
    select = jnp.where(index == token, 1.0, 0.0).astype(BF16)
    out_ref[...] = (hidden_ref[0:128].astype(F32) + dot(select, rows, TN)).astype(BF16)


def shards(
    atoms,
    atom_bias,
    key_shift,
    atom_token,
    token_atoms,
    token_mask,
    pair,
    w_atom_qkv,
    w_atom_out,
    w_pool,
    w_token_qkv,
    w_token_out,
    w_bias,
    w_back,
    cotangent,
):
    row_count, col_count = lax.axis_size("row"), lax.axis_size("col")
    devices = row_count * col_count
    core_pairs = [(i, i ^ 1) for i in range(col_count)]
    chip_pairs = [(i, i + 1) for i in range(1, devices - 1, 2)]
    chip_pairs = chip_pairs + [(j, i) for i, j in chip_pairs]

    def chip_shift(steps):
        return [(i, (i + 2 * steps) % col_count) for i in range(col_count)]

    tokens = atom_token.reshape(1, 128)
    payload = jax.ShapeDtypeStruct((464, 128), BF16)
    near, far, side = pl.pallas_call(
        pack_kernel,
        in_specs=[SMEM] * 3 + [VMEM] * 4,
        out_specs=[VMEM] * 3,
        out_shape=[payload, payload, pltpu.VMEM((48, 128), F32)],
        compiler_params=params(4),
        name="pack",
        cost_estimate=pl.CostEstimate(flops=0, bytes_accessed=1 << 20, transcendentals=0),
    )(
        outside(key_shift),
        outside(token_atoms),
        outside(token_mask),
        outside(atoms),
        outside(atom_bias),
        outside(cotangent),
        outside(tokens),
    )
    near = lax.ppermute(near, "col", core_pairs)
    far = lax.ppermute(far, ("row", "col"), chip_pairs)

    tile = pair.reshape(128, 256, 128)
    head_rows = jnp.repeat(jnp.transpose(w_bias), GROUP, axis=0)
    def pair_bias(first, groups, name, *brought):
        return pl.pallas_call(
            functools.partial(pair_bias_kernel, first),
            in_specs=[HBM, VMEM] + [HBM] * len(brought),
            out_specs=[HBM] + [VMEM] * len(brought),
            out_shape=[pltpu.HBM((groups, HT, GROUP, 256), F32)]
            + [pltpu.VMEM(value.shape, value.dtype) for value in brought],
            scratch_shapes=[
                pltpu.VMEM((groups * GROUP, 256, 128), BF16),
                pltpu.VMEM((groups, HT, GROUP, 256), F32),
                pltpu.SemaphoreType.DMA((groups,)),
                pltpu.SemaphoreType.DMA((groups,)),
                pltpu.SemaphoreType.DMA((max(len(brought), 1),)),
            ],
            compiler_params=params(14),
            name=name,
            cost_estimate=pl.CostEstimate(
                flops=groups << 26, bytes_accessed=groups << 19, transcendentals=0
            ),
        )(outside(tile), head_rows, *[outside(value) for value in brought])

    half = EARLY
    early, *atom_inputs = pair_bias(
        0,
        half,
        "pair_bias_early",
        atoms,
        atom_bias,
        cotangent,
        w_atom_qkv,
        w_atom_out,
        w_pool,
    )
    (late,) = pair_bias(half, 16 - half, "pair_bias_late")

    hidden, pooled, to_row, to_col, token_kv = pl.pallas_call(
        atom_kernel,
        in_specs=[VMEM] * 9 + [HBM],
        out_specs=[VMEM] * 5,
        out_shape=[
            pltpu.VMEM((144, 128), BF16),
            pltpu.HBM((16, 768), F32),
            pltpu.VMEM((row_count, 16, 768), BF16),
            pltpu.VMEM((16, 896), BF16),
            pltpu.VMEM((768, 1536), BF16),
        ],
        scratch_shapes=[
            pltpu.VMEM((464, 128), BF16),
            pltpu.VMEM((464, 128), BF16),
            pltpu.SemaphoreType.DMA((4,)),
        ],
        compiler_params=params(8),
        name="atom_stage",
        cost_estimate=pl.CostEstimate(flops=1 << 28, bytes_accessed=2 << 20, transcendentals=1 << 17),
    )(
        inside(side),
        near,
        far,
        *[inside(value) for value in atom_inputs],
        outside(w_token_qkv),
    )
    partner = lax.ppermute(to_col, "col", core_pairs)
    keys = lax.all_to_all(to_row, "row", 0, 0).reshape(256, 768)
    own = pl.pallas_call(
        stack_kernel,
        in_specs=[VMEM] * 2,
        out_specs=VMEM,
        out_shape=pltpu.VMEM((2, 16, 896), BF16),
        compiler_params=params(4),
        name="stack",
        cost_estimate=pl.CostEstimate(flops=1 << 32, bytes_accessed=1 << 18, transcendentals=0),
    )(inside(to_col), partner)
    shifted = [lax.ppermute(own, "col", chip_shift(s)) for s in range(1, 4)]

    stat = pltpu.VMEM((128, 128), F32)
    swapped = jax.ShapeDtypeStruct((4, 16, 1024), BF16)
    folded = jax.ShapeDtypeStruct((16, 1792), BF16)
    table = pltpu.VMEM((16, HT, GROUP, 256), F32)
    prob, grad, stats, keep, give, pooled, token_out, back = pl.pallas_call(
        token_kernel,
        in_specs=[VMEM] * 5 + [HBM] * 2 + [VMEM] + [HBM] * 4,
        out_specs=[VMEM] * 8,
        scratch_shapes=[
            pltpu.VMEM((128, 896), BF16),
            pltpu.VMEM((128, 768), F32),
            pltpu.VMEM((768, 768), BF16),
            pltpu.VMEM((16, HT, GROUP, 256), F32),
            pltpu.SemaphoreType.DMA((10,)),
        ],
        out_shape=[
            table,
            table,
            stat,
            pltpu.VMEM((4, 16, 768), F32),
            swapped,
            pltpu.VMEM((16, 768), F32),
            pltpu.VMEM(w_token_out.shape, BF16),
            pltpu.VMEM(w_back.shape, BF16),
        ],
        compiler_params=params(16),
        name="token_stage",
        cost_estimate=pl.CostEstimate(flops=1 << 31, bytes_accessed=12 << 20, transcendentals=1 << 19),
    )(
        inside(keys),
        inside(own),
        *shifted,
        outside(early),
        outside(late),
        inside(token_kv),
        outside(w_token_qkv),
        outside(w_token_out),
        outside(w_back),
        outside(pooled),
    )
    given = lax.ppermute(give, "col", core_pairs)
    *sent, mixed, joint = pl.pallas_call(
        fold_kernel,
        in_specs=[VMEM] * 3,
        out_specs=[VMEM] * 5,
        out_shape=[folded, folded, folded, pltpu.VMEM((16, 768), F32), stat],
        scratch_shapes=[pltpu.VMEM((2, 128, 128), F32), pltpu.VMEM((4, 16, 768), F32)],
        compiler_params=params(6),
        name="fold",
        cost_estimate=pl.CostEstimate(flops=1 << 26, bytes_accessed=2 << 20, transcendentals=1 << 17),
    )(inside(keep), inside(stats), given)
    parts = [lax.ppermute(part, "col", chip_shift(s + 1)) for s, part in enumerate(sent)]

    scale, diag, low, near, far = pl.pallas_call(
        merge_kernel,
        in_specs=[VMEM] * 9,
        out_specs=[VMEM] * 5,
        out_shape=[
            stat,
            stat,
            pltpu.VMEM((2, 16, 128), BF16),
            jax.ShapeDtypeStruct((16, 128), BF16),
            jax.ShapeDtypeStruct((16, 128), BF16),
        ],
        scratch_shapes=[pltpu.VMEM((4, 128, 128), F32)],
        compiler_params=params(6),
        name="merge",
        cost_estimate=pl.CostEstimate(flops=1 << 26, bytes_accessed=2 << 20, transcendentals=1 << 17),
    )(
        inside(stats),
        inside(mixed),
        inside(joint),
        *parts,
        inside(pooled),
        inside(token_out),
        inside(back),
    )
    near = lax.ppermute(near, "col", core_pairs)
    far = lax.ppermute(far, ("row", "col"), chip_pairs)

    pair_grad = pl.pallas_call(
        pair_grad_kernel,
        in_specs=[VMEM] * 5,
        out_specs=HBM,
        out_shape=jax.ShapeDtypeStruct((128, 256, 128), BF16),
        scratch_shapes=[pltpu.VMEM((128, 256, 128), BF16), pltpu.SemaphoreType.DMA((16,))],
        compiler_params=params(14),
        name="pair_grad",
        cost_estimate=pl.CostEstimate(
            flops=2 * 128 * 256 * 128 * 16 * 8, bytes_accessed=14 << 20, transcendentals=0
        ),
    )(inside(prob), inside(grad), inside(scale), inside(diag), head_rows)
    atom_out = pl.pallas_call(
        atom_out_kernel,
        in_specs=[VMEM] * 4,
        out_specs=VMEM,
        out_shape=jax.ShapeDtypeStruct((128, 128), BF16),
        compiler_params=params(4),
        name="atom_out",
        cost_estimate=pl.CostEstimate(flops=1 << 21, bytes_accessed=1 << 17, transcendentals=0),
    )(near, far, inside(low), inside(hidden))
    return (atom_out, pair_grad.reshape(pair.shape))


def solution(mesh):
    return jax.shard_map(
        shards,
        mesh=mesh,
        in_specs=(
            P(("row", "col"), None),
            P(None, ("row", "col"), None),
            P(("row", "col")),
            P(("row", "col")),
            P(("row", "col")),
            P(("row", "col")),
            P("row", None, "col", None, None),
            P(),
            P(),
            P(),
            P(),
            P(),
            P(),
            P(),
            P(("row", "col"), None),
        ),
        out_specs=(P(("row", "col"), None), P("row", None, "col", None, None)),
        check_vma=False,
    )
```

```python
import functools
import math

import jax
import jax.numpy as jnp
from jax import lax
from jax.experimental import pallas as pl
from jax.experimental.pallas import tpu as pltpu
from jax.sharding import PartitionSpec as P

HA = 4
HT = 16
QB = 32
KW = 128
SHIFT = 16
HALF = 64
GATHER_SHIFTS = (1, 3, 2)
FOLD_SHIFTS = (2, 1, 3)
EARLY = 8
GROUP = 8
AUX = 16
EPSILON = 1e-05
LOWEST = -1e30
MASKED = 1024.0
F32 = jnp.float32
BF16 = jnp.bfloat16
NT = (((1,), (1,)), ((), ()))
TN = (((0,), (0,)), ((), ()))

VMEM = pl.BlockSpec(memory_space=pltpu.VMEM)
HBM = pl.BlockSpec(memory_space=pltpu.HBM)
SMEM = pl.BlockSpec(memory_space=pltpu.SMEM)


def params(mib):
    return pltpu.CompilerParams(vmem_limit_bytes=mib << 20)


def outside(value):
    return pltpu.with_memory_space_constraint(value, pltpu.HBM)


def inside(value):
    return pltpu.with_memory_space_constraint(value, pltpu.VMEM)


def place():
    return lax.axis_index("row"), lax.axis_index("col")


def iota(shape, dim):
    return lax.broadcasted_iota(jnp.int32, shape, dim)


def dot(a, b, dims=None):
    if dims is None:
        return jnp.dot(a, b, preferred_element_type=F32)
    return lax.dot_general(a, b, dims, preferred_element_type=F32)


def normal(values):
    centred = values - jnp.mean(values, axis=-1, keepdims=True)
    return centred * lax.rsqrt(jnp.mean(centred * centred, axis=-1, keepdims=True) + EPSILON)


def split(values):
    high = values.astype(BF16)
    return high, (values - high.astype(F32)).astype(BF16)


def grouped_weight(head_rows, member):
    rows = iota(head_rows.shape, 0)
    return jnp.where(rows % GROUP == member, head_rows, 0.0).astype(BF16)


def pair_bias_kernel(first, pair_ref, head_ref, *refs):
    *brought, tile_ref, bias_ref, arrived, left, came = refs
    extra = len(brought) // 2
    out_ref = brought[extra]
    extras = [
        pltpu.make_async_copy(brought[n], brought[extra + 1 + n], came.at[n]) for n in range(extra)
    ]
    groups = out_ref.shape[0]
    window = min(8, groups)

    def copy(g):
        rows = pl.ds(g * GROUP, GROUP)
        here = pl.ds((g + first) * GROUP, GROUP)
        return pltpu.make_async_copy(pair_ref.at[here], tile_ref.at[rows], arrived.at[g])

    def leave(g):
        return pltpu.make_async_copy(bias_ref.at[g], out_ref.at[g], left.at[g])

    for g in range(window):
        copy(g).start()
    for extra_copy in extras:
        extra_copy.start()
    weight = head_ref[...].astype(F32).reshape(HT, GROUP, 128)[:, 0].astype(BF16)

    def step(g, carry):
        copy(g).wait()
        if window < groups:

            @pl.when(g + window < groups)
            def _():
                copy(g + window).start()

        for i in range(GROUP):
            bias_ref[g, :, i, :] = dot(weight, tile_ref[g * GROUP + i], NT)
        leave(g).start()
        return carry

    lax.fori_loop(0, groups, step, 0, unroll=groups)
    for g in range(groups):
        leave(g).wait()
    for extra_copy in extras:
        extra_copy.wait()


def pack_kernel(
    shift_ref,
    count_ref,
    mask_ref,
    atoms_ref,
    bias_ref,
    cot_ref,
    token_ref,
    near_ref,
    far_ref,
    side_ref,
):
    row, col = place()
    odd = lax.rem(col, 2)
    line = iota((AUX, 128), 0)
    device = row * lax.axis_size("col") + col
    aux = jnp.where(line == 0, token_ref[...] - (16 * device - 17), 0)
    for n in range(4):
        aux = jnp.where(line == 1 + n, shift_ref[n], aux)
    wide = aux.astype(F32)
    aux = wide.astype(BF16)

    def fill(out_ref, at):
        out_ref[0:128] = atoms_ref[...]
        for h in range(HA):
            out_ref[128 + HALF * h : 128 + HALF * (h + 1)] = bias_ref[h, at : at + HALF]
        out_ref[384:448] = cot_ref[at : at + HALF]
        out_ref[448:464] = aux

    side_ref[0:16] = wide
    count = jnp.zeros((16, 128), jnp.int32)
    live = jnp.zeros((16, 128), jnp.int32)
    for t in range(16):
        count = jnp.where(line == t, count_ref[t], count)
        live = jnp.where(line == t, mask_ref[t], live)
    side_ref[16:32] = count.astype(F32)
    side_ref[32:48] = live.astype(F32)

    @pl.when(odd == 1)
    def _():
        fill(near_ref, 0)
        fill(far_ref, HALF)

    @pl.when(odd == 0)
    def _():
        fill(near_ref, HALF)
        fill(far_ref, 0)


def atom_kernel(
    side_ref,
    near_ref,
    far_ref,
    atoms_ref,
    bias_ref,
    cot_ref,
    w_qkv_ref,
    w_out_ref,
    w_pool_ref,
    token_qkv_ref,
    hidden_ref,
    pooled_ref,
    to_row_ref,
    to_col_ref,
    token_kv_ref,
    prev_ref,
    next_ref,
    arrived,
):
    copies = []
    for n in range(4):
        rows = slice(192 * n, 192 * (n + 1))
        copies.append(
            pltpu.make_async_copy(
                token_qkv_ref.at[rows, 768:2304], token_kv_ref.at[rows], arrived.at[n]
            )
        )
    for copy in copies:
        copy.start()
    row, col = place()
    odd = lax.rem(col, 2)
    device = row * lax.axis_size("col") + col
    atom_count = 128 * lax.axis_size("row") * lax.axis_size("col")

    @pl.when(odd == 1)
    def _():
        prev_ref[...] = near_ref[...]
        next_ref[...] = far_ref[...]

    @pl.when(odd == 0)
    def _():
        prev_ref[...] = far_ref[...]
        next_ref[...] = near_ref[...]

    first = device * 128
    extended = jnp.concatenate([prev_ref[0:128], atoms_ref[...], next_ref[0:128]], axis=0)
    wide = extended.astype(F32)
    project = dot(normal(wide).astype(BF16), w_qkv_ref[...]).astype(BF16)
    head_lane = iota((QB, 128), 1) // 32
    head_mask = [jnp.where(head_lane == h, 1.0, 0.0) for h in range(HA)]
    slot = iota((1, KW), 1)
    offset = iota((KW, 160), 1) - iota((KW, 160), 0) - SHIFT
    order = (2, 3, 4, 5, 6, 7, 0, 1)
    biases, shifts, windows, stacks = [], [], [], []
    for block in order:
        if block < 2:
            source, local = prev_ref, block
            shift = prev_ref[451 + local : 452 + local].astype(F32).astype(jnp.int32)
        elif block > 5:
            source, local = next_ref, block - 6
            shift = next_ref[449 + local : 450 + local].astype(F32).astype(jnp.int32)
        else:
            source, local = None, block - 2
            shift = side_ref[1 + local : 2 + local].astype(jnp.int32)
        for h in range(HA):
            if source is None:
                biases.append(bias_ref[h, 32 * local : 32 * local + 32])
            else:
                at = 128 + HALF * h + 32 * local
                biases.append(source[at : at + 32])
        shifts.append(shift)
    for block, shift in zip(order, shifts):
        pick = jnp.where(offset == shift[:, 0:1], 1.0, 0.0).astype(BF16)
        windows.append(dot(pick, project[32 * block : 32 * block + 160, 128:]).astype(BF16))
        query = project[64 + 32 * block : 96 + 32 * block, :128].astype(F32)
        stacks.append(
            jnp.concatenate([query * head_mask[h] for h in range(HA)], axis=0).astype(BF16)
        )
    scores = [
        dot(stack, window[:, :128], NT) * (1.0 / math.sqrt(32))
        for stack, window in zip(stacks, windows)
    ]
    weights = []
    for n, block in enumerate(order):
        score = scores[n] + jnp.concatenate(biases[HA * n : HA * n + HA], axis=0).astype(F32)
        position = slot + (first + 32 * block - 112) + shifts[n]
        inside = (position >= 0) & (position < atom_count)
        score = jnp.where(inside, score, LOWEST)
        raised = jnp.exp(score - jnp.max(score, axis=-1, keepdims=True))
        weights.append((raised / jnp.sum(raised, axis=-1, keepdims=True)).astype(BF16))
    mixes = []
    for weight, window in zip(weights, windows):
        mixed = dot(weight, window[:, 128:])
        mix = mixed[0:32] * head_mask[0]
        for h in range(1, HA):
            mix = mix + mixed[32 * h : 32 * h + 32] * head_mask[h]
        mixes.append(mix)
    mixture = jnp.concatenate(mixes, axis=0).astype(BF16)
    base = jnp.concatenate([wide[128:320], wide[64:128]], axis=0)
    hidden = (base + dot(mixture, w_out_ref[...])).astype(BF16)
    hidden_ref[0:128] = hidden[:128]
    relative = side_ref[0:1] - 1.0
    hidden_ref[128:144] = jnp.broadcast_to(relative, (16, 128)).astype(BF16)
    lifted = jnp.maximum(dot(hidden, w_pool_ref[...]), 0.0)
    own_token = side_ref[0:1] - 17.0
    prev_token = prev_ref[448:449].astype(F32) - 33.0
    next_token = next_ref[448:449].astype(F32) - 1.0
    beside = jnp.where(iota((1, 128), 1) < HALF, next_token, prev_token)
    token = jnp.concatenate([own_token, beside], axis=1)
    select = jnp.where(iota((16, 256), 0).astype(F32) == token, 1.0, 0.0).astype(BF16)
    high, low = split(lifted)
    count = jnp.concatenate([side_ref[16:32]] * 6, axis=1)
    pooled = (dot(select, high) + dot(select, low)) / count
    pooled_ref[...] = pooled
    normed = normal(pooled).astype(BF16)
    cot = jnp.concatenate([cot_ref[...], next_ref[384:448], prev_ref[384:448]], axis=0)
    grad_up = dot(select, cot).astype(BF16)
    live = jnp.concatenate([side_ref[32:48]] * 6, axis=1)
    marked = jnp.where(live > 0, normed.astype(F32), MASKED).astype(BF16)
    for r in range(to_row_ref.shape[0]):
        to_row_ref[r] = marked
    to_col_ref[:, :768] = normed
    to_col_ref[:, 768:] = grad_up
    for copy in copies:
        copy.wait()


def window_of(head):
    block, rest = divmod(head, 8)
    return 384 * block + (0 if rest < 5 else 128)


def stack_kernel(own_ref, partner_ref, out_ref):
    row, col = place()
    core = lax.rem(col, 2)
    out_ref[core] = own_ref[...]
    out_ref[1 - core] = partner_ref[...]


def token_kernel(
    keys_ref,
    own_ref,
    first_ref,
    second_ref,
    third_ref,
    early_ref,
    late_ref,
    w_kv_ref,
    w_qkv_ref,
    w_out_ref,
    w_back_ref,
    pooled_ref,
    prob_ref,
    grad_ref,
    stats_ref,
    keep_ref,
    give_ref,
    pooled_out_ref,
    inner_out_ref,
    inner_back_ref,
    rows_ref,
    mixed_ref,
    inner_ref,
    bias_ref,
    arrived,
):
    copies = []
    for n in range(2):
        rows = slice(384 * n, 384 * (n + 1))
        copies.append((w_qkv_ref.at[rows, 0:768], inner_ref.at[rows]))
    copies.append((w_back_ref, inner_back_ref))
    for n in range(2):
        rows = slice(384 * n, 384 * (n + 1))
        copies.append((w_out_ref.at[rows], inner_out_ref.at[rows]))
    early = early_ref.shape[0]
    for first, count, source in ((0, early, early_ref), (early, 16 - early, late_ref)):
        for start, stop in ((0, count // 2), (count // 2, count)):
            copies.append(
                (source.at[start:stop], bias_ref.at[first + start : first + stop])
            )
    copies.append((pooled_ref, pooled_out_ref))
    copies = [pltpu.make_async_copy(a, b, arrived.at[n]) for n, (a, b) in enumerate(copies)]
    for copy in copies[:5]:
        copy.start()

    row, col = place()
    chip, core = lax.div(col, 2), lax.rem(col, 2)
    parts = (own_ref, first_ref, second_ref, third_ref)
    for s, part_ref in zip((0,) + GATHER_SHIFTS, parts):
        there = lax.rem(chip + 4 - s, 4) * 32
        rows_ref[pl.ds(pl.multiple_of(there, 32), 16)] = part_ref[0]
        rows_ref[pl.ds(pl.multiple_of(there + 16, 16), 16)] = part_ref[1]
    key = dot(keys_ref[...], w_kv_ref[:, :768]).astype(BF16)
    value = dot(keys_ref[...], w_kv_ref[:, 768:]).astype(BF16)
    for copy in copies[5:]:
        copy.start()
    for copy in copies[:2]:
        copy.wait()
    query = dot(rows_ref[:, :768], inner_ref[...]).astype(BF16)
    for copy in copies[2:5]:
        copy.wait()
    middle = dot(rows_ref[:, 768:], inner_back_ref[...], NT).astype(BF16)
    grad = dot(middle, inner_out_ref[...], NT).astype(BF16)
    first = keys_ref[:, :128].astype(F32).T[0:1]
    closed = jnp.where(first < MASKED, 0.0, -jnp.inf)
    lane = iota((128, 256), 1)
    stat_lane = iota((128, 128), 1)

    def within(h):
        at = window_of(h)
        return (lane >= 48 * h - at) & (lane < 48 * (h + 1) - at)

    for h in range(HT):
        at = window_of(h)
        grad_h = jnp.where(within(h), grad[:, at : at + 256].astype(F32), 0.0).astype(BF16)
        grads = dot(grad_h, value[:, at : at + 256], NT)
        grad_ref[:, h] = grads.reshape(16, GROUP, 256)
    for copy in copies[5:]:
        copy.wait()
    for h in range(HT):
        at = window_of(h)
        query_h = jnp.where(within(h), query[:, at : at + 256].astype(F32), 0.0).astype(BF16)
        scores = dot(query_h, key[:, at : at + 256], NT) * (1.0 / math.sqrt(48))
        bias = bias_ref[:, h].reshape(128, 256)
        prob_ref[:, h] = (scores + bias + closed).reshape(16, GROUP, 256)
    tops = jnp.zeros((128, 128), F32)
    sums = jnp.zeros((128, 128), F32)
    diags = jnp.zeros((128, 128), F32)
    for h in range(HT):
        scores = prob_ref[:, h].reshape(128, 256)
        top = jnp.maximum(jnp.max(scores, axis=-1, keepdims=True), LOWEST)
        high = top.astype(BF16).astype(F32)
        top = high + (top - high).astype(BF16).astype(F32)
        raised = jnp.exp(scores - top)
        prob_ref[:, h] = raised.reshape(16, GROUP, 256)
        total = jnp.sum(raised, axis=-1, keepdims=True)
        diag = jnp.sum(raised * grad_ref[:, h].reshape(128, 256), axis=-1, keepdims=True)
        here = stat_lane == h
        tops = jnp.where(here, top, tops)
        sums = jnp.where(here, total, sums)
        diags = jnp.where(here, diag, diags)
    for at in (0, 128, 384, 512):
        out = None
        for h in range(HT):
            if window_of(h) == at:
                raised = prob_ref[:, h].reshape(128, 256).astype(BF16)
                part = jnp.where(within(h), dot(raised, value[:, at : at + 256]), 0.0)
                out = part if out is None else out + part
        if at % 384 == 0:
            mixed_ref[:, at : at + 256] = out
        else:
            mixed_ref[:, at : at + 128] = mixed_ref[:, at : at + 128] + out[:, :128]
            mixed_ref[:, at + 128 : at + 256] = out[:, 128:]
    stats_ref[...] = tops + pltpu.roll(sums, 32, axis=1) + pltpu.roll(diags, 64, axis=1)
    packed = packed_stats(tops, sums, diags)
    for n in range(4):
        there = 32 * n + 16 * core
        keep_ref[n] = mixed_ref[pl.ds(pl.multiple_of(there, 16), 16)]
        there = 32 * n + 16 - 16 * core
        part = mixed_ref[pl.ds(pl.multiple_of(there, 16), 16)]
        give_ref[n, :, :768] = part.astype(BF16)
        for k in range(2):
            at = 32 * n + 16 * k
            give_ref[n, :, 768 + 128 * k : 896 + 128 * k] = packed[at : at + 16]


def packed_stats(tops, sums, diags):
    stats = jnp.zeros((128, 128), F32)
    for k, part in enumerate((tops, sums, diags)):
        high = part.astype(BF16).astype(F32)
        for n, piece in enumerate((high, part - high)):
            turn = 32 * k + 16 * n
            stats = stats + (pltpu.roll(piece, turn, axis=1) if turn else piece)
    return stats.astype(BF16)


def spread_heads(factors):
    spread = jnp.where(iota((128, 768), 1) // 48 == iota((128, 768), 0), 1.0, 0.0).astype(BF16)
    high, low = split(factors)
    return dot(high, spread) + dot(low, spread)


def parted_stats(stats):
    lane = iota((128, 128), 1)
    parts = [stats, pltpu.roll(stats, 96, axis=1), pltpu.roll(stats, 64, axis=1)]
    return [jnp.where(lane < HT, part, 0.0) for part in parts]


def fold_kernel(
    keep_ref,
    stats_ref,
    given_ref,
    first_ref,
    second_ref,
    third_ref,
    own_ref,
    joint_ref,
    ratio_ref,
    mixed_ref,
):
    row, col = place()
    chip, core = lax.div(col, 2), lax.rem(col, 2)
    given = jnp.concatenate(
        [given_ref[n, :, 768 + 128 * k : 896 + 128 * k] for n in range(4) for k in range(2)],
        axis=0,
    ).astype(F32)
    given = given + pltpu.roll(given, 112, axis=1)
    sides = [parted_stats(stats_ref[...]), parted_stats(given)]
    top = jnp.maximum(sides[0][0], sides[1][0])
    ratios = [jnp.exp(side[0] - top) for side in sides]
    total = ratios[0] * sides[0][1] + ratios[1] * sides[1][1]
    diag = ratios[0] * sides[0][2] + ratios[1] * sides[1][2]
    joint_ref[...] = top + pltpu.roll(total, 32, axis=1) + pltpu.roll(diag, 64, axis=1)
    ratio_ref[0] = ratios[0]
    ratio_ref[1] = ratios[1]
    rows = [pl.ds(pl.multiple_of(32 * n + 16 * core, 16), 16) for n in range(4)]
    factors = spread_heads(
        jnp.concatenate([ratio_ref[side, rows[n]] for side in range(2) for n in range(4)], axis=0)
    )
    for n in range(4):
        given_n = given_ref[n, :, :768].astype(F32)
        mixed_ref[n] = (
            keep_ref[n] * factors[16 * n : 16 * n + 16]
            + given_n * factors[64 + 16 * n : 80 + 16 * n]
        )
    packed = packed_stats(top, total, diag)
    for s, out_ref in zip(FOLD_SHIFTS, (first_ref, second_ref, third_ref)):
        out_ref[:, :768] = mixed_ref[lax.rem(chip + s, 4)].astype(BF16)
        for k in range(8):
            out_ref[:, 768 + 128 * k : 896 + 128 * k] = packed[16 * k : 16 * k + 16]
    own_ref[...] = mixed_ref[chip]


def merge_kernel(
    stats_ref,
    own_ref,
    joint_ref,
    first_ref,
    second_ref,
    third_ref,
    pooled_ref,
    w_out_ref,
    w_back_ref,
    scale_ref,
    diag_ref,
    low_ref,
    near_ref,
    far_ref,
    ratio_ref,
):
    row, col = place()
    lane = iota((128, 128), 1)
    sides = [parted_stats(joint_ref[...])]
    for part_ref in (first_ref, second_ref, third_ref):
        stats = jnp.concatenate(
            [part_ref[:, 768 + 128 * k : 896 + 128 * k] for k in range(8)], axis=0
        ).astype(F32)
        sides.append(parted_stats(stats + pltpu.roll(stats, 112, axis=1)))
    top = functools.reduce(jnp.maximum, [side[0] for side in sides])
    ratios = [jnp.exp(side[0] - top) for side in sides]
    total = functools.reduce(jnp.add, [r * side[1] for r, side in zip(ratios, sides)])
    diag = functools.reduce(jnp.add, [r * side[2] for r, side in zip(ratios, sides)])
    inverse = 1.0 / jnp.where(lane < HT, total, 1.0)
    for n in range(4):
        ratio_ref[n] = ratios[n] * inverse
    own_top = parted_stats(stats_ref[...])[0]
    scale_ref[...] = jnp.exp(own_top - top) * inverse
    diag_ref[...] = diag * inverse
    rows = pl.ds(pl.multiple_of(col * 16, 16), 16)
    factors = spread_heads(jnp.concatenate([ratio_ref[n, rows] for n in range(4)], axis=0))
    mixed = own_ref[...] * factors[0:16]
    for n, part_ref in enumerate((first_ref, second_ref, third_ref)):
        mixed = mixed + part_ref[:, :768].astype(F32) * factors[16 * n + 16 : 16 * n + 32]
    updated = (pooled_ref[...] + dot(mixed.astype(BF16), w_out_ref[...])).astype(BF16)
    high, low = split(dot(updated, w_back_ref[...]))
    near_ref[...] = high
    far_ref[...] = high
    low_ref[0] = high
    low_ref[1] = low


def pair_grad_kernel(prob_ref, grad_ref, scale_ref, diag_ref, head_ref, out_ref, tile_ref, left):
    groups = prob_ref.shape[0]

    def copy(g):
        rows = pl.ds(g * GROUP, GROUP)
        return pltpu.make_async_copy(tile_ref.at[rows], out_ref.at[rows], left.at[g])

    head_rows = head_ref[...].astype(F32)
    weights = jnp.concatenate([grouped_weight(head_rows, i) for i in range(GROUP)], axis=1)

    def score_of(g):
        rows = pl.ds(pl.multiple_of(g * GROUP, GROUP), GROUP)
        scale = scale_ref[rows]
        diag = diag_ref[rows]
        score = jnp.concatenate(
            [
                prob_ref[g, h] * scale[:, h : h + 1] * (grad_ref[g, h] - diag[:, h : h + 1])
                for h in range(HT)
            ],
            axis=0,
        )
        return score.T.astype(BF16)

    def step(g, score):
        following = score_of(jnp.minimum(g + 1, groups - 1))
        result = dot(score, weights)
        for i in range(GROUP):
            tile_ref[g * GROUP + i] = result[:, 128 * i : 128 * (i + 1)].astype(BF16)
        copy(g).start()
        return following

    lax.fori_loop(0, groups, step, score_of(0), unroll=groups)
    for g in range(groups):
        copy(g).wait()


def atom_out_kernel(far_ref, near_ref, low_ref, hidden_ref, out_ref):
    row, col = place()
    odd = lax.rem(col, 2) == 1
    near = near_ref[...].astype(F32)
    far = far_ref[...].astype(F32)
    before = jnp.where(odd, near, far).astype(BF16)
    after = jnp.where(odd, far, near).astype(BF16)
    rows = jnp.concatenate([before, low_ref[0], after, low_ref[1]], axis=0)
    token = hidden_ref[128:144].astype(F32)[0:1]
    index = iota((64, 128), 0)
    index = jnp.where(index < 48, index, index - 32).astype(F32)
    select = jnp.where(index == token, 1.0, 0.0).astype(BF16)
    out_ref[...] = (hidden_ref[0:128].astype(F32) + dot(select, rows, TN)).astype(BF16)


def shards(
    atoms,
    atom_bias,
    key_shift,
    atom_token,
    token_atoms,
    token_mask,
    pair,
    w_atom_qkv,
    w_atom_out,
    w_pool,
    w_token_qkv,
    w_token_out,
    w_bias,
    w_back,
    cotangent,
):
    row_count, col_count = lax.axis_size("row"), lax.axis_size("col")
    devices = row_count * col_count
    core_pairs = [(i, i ^ 1) for i in range(col_count)]
    chip_pairs = [(i, i + 1) for i in range(1, devices - 1, 2)]
    chip_pairs = chip_pairs + [(j, i) for i, j in chip_pairs]

    def chip_shift(steps):
        return [(i, (i + 2 * steps) % col_count) for i in range(col_count)]

    tokens = atom_token.reshape(1, 128)
    payload = jax.ShapeDtypeStruct((464, 128), BF16)
    near, far, side = pl.pallas_call(
        pack_kernel,
        in_specs=[SMEM] * 3 + [VMEM] * 4,
        out_specs=[VMEM] * 3,
        out_shape=[payload, payload, pltpu.VMEM((48, 128), F32)],
        compiler_params=params(4),
        name="pack",
        cost_estimate=pl.CostEstimate(flops=0, bytes_accessed=1 << 20, transcendentals=0),
    )(
        outside(key_shift),
        outside(token_atoms),
        outside(token_mask),
        outside(atoms),
        outside(atom_bias),
        outside(cotangent),
        outside(tokens),
    )
    near = lax.ppermute(near, "col", core_pairs)
    far = lax.ppermute(far, ("row", "col"), chip_pairs)

    tile = pair.reshape(128, 256, 128)
    head_rows = jnp.repeat(jnp.transpose(w_bias), GROUP, axis=0)
    def pair_bias(first, groups, name, *brought):
        return pl.pallas_call(
            functools.partial(pair_bias_kernel, first),
            in_specs=[HBM, VMEM] + [HBM] * len(brought),
            out_specs=[HBM] + [VMEM] * len(brought),
            out_shape=[pltpu.HBM((groups, HT, GROUP, 256), F32)]
            + [pltpu.VMEM(value.shape, value.dtype) for value in brought],
            scratch_shapes=[
                pltpu.VMEM((groups * GROUP, 256, 128), BF16),
                pltpu.VMEM((groups, HT, GROUP, 256), F32),
                pltpu.SemaphoreType.DMA((groups,)),
                pltpu.SemaphoreType.DMA((groups,)),
                pltpu.SemaphoreType.DMA((max(len(brought), 1),)),
            ],
            compiler_params=params(14),
            name=name,
            cost_estimate=pl.CostEstimate(
                flops=groups << 26, bytes_accessed=groups << 19, transcendentals=0
            ),
        )(outside(tile), head_rows, *[outside(value) for value in brought])

    half = EARLY
    early, *atom_inputs = pair_bias(
        0,
        half,
        "pair_bias_early",
        atoms,
        atom_bias,
        cotangent,
        w_atom_qkv,
        w_atom_out,
        w_pool,
    )
    (late,) = pair_bias(half, 16 - half, "pair_bias_late")

    hidden, pooled, to_row, to_col, token_kv = pl.pallas_call(
        atom_kernel,
        in_specs=[VMEM] * 9 + [HBM],
        out_specs=[VMEM] * 5,
        out_shape=[
            pltpu.VMEM((144, 128), BF16),
            pltpu.HBM((16, 768), F32),
            pltpu.VMEM((row_count, 16, 768), BF16),
            pltpu.VMEM((16, 896), BF16),
            pltpu.VMEM((768, 1536), BF16),
        ],
        scratch_shapes=[
            pltpu.VMEM((464, 128), BF16),
            pltpu.VMEM((464, 128), BF16),
            pltpu.SemaphoreType.DMA((4,)),
        ],
        compiler_params=params(8),
        name="atom_stage",
        cost_estimate=pl.CostEstimate(flops=1 << 28, bytes_accessed=2 << 20, transcendentals=1 << 17),
    )(
        inside(side),
        near,
        far,
        *[inside(value) for value in atom_inputs],
        outside(w_token_qkv),
    )
    partner = lax.ppermute(to_col, "col", core_pairs)
    keys = lax.all_to_all(to_row, "row", 0, 0).reshape(256, 768)
    own = pl.pallas_call(
        stack_kernel,
        in_specs=[VMEM] * 2,
        out_specs=VMEM,
        out_shape=pltpu.VMEM((2, 16, 896), BF16),
        compiler_params=params(4),
        name="stack",
        cost_estimate=pl.CostEstimate(flops=1 << 32, bytes_accessed=1 << 18, transcendentals=0),
    )(inside(to_col), partner)
    shifted = [lax.ppermute(own, "col", chip_shift(s)) for s in GATHER_SHIFTS]

    stat = pltpu.VMEM((128, 128), F32)
    swapped = jax.ShapeDtypeStruct((4, 16, 1024), BF16)
    folded = jax.ShapeDtypeStruct((16, 1792), BF16)
    table = pltpu.VMEM((16, HT, GROUP, 256), F32)
    prob, grad, stats, keep, give, pooled, token_out, back = pl.pallas_call(
        token_kernel,
        in_specs=[VMEM] * 5 + [HBM] * 2 + [VMEM] + [HBM] * 4,
        out_specs=[VMEM] * 8,
        scratch_shapes=[
            pltpu.VMEM((128, 896), BF16),
            pltpu.VMEM((128, 768), F32),
            pltpu.VMEM((768, 768), BF16),
            pltpu.VMEM((16, HT, GROUP, 256), F32),
            pltpu.SemaphoreType.DMA((10,)),
        ],
        out_shape=[
            table,
            table,
            stat,
            pltpu.VMEM((4, 16, 768), F32),
            swapped,
            pltpu.VMEM((16, 768), F32),
            pltpu.VMEM(w_token_out.shape, BF16),
            pltpu.VMEM(w_back.shape, BF16),
        ],
        compiler_params=params(16),
        name="token_stage",
        cost_estimate=pl.CostEstimate(flops=1 << 31, bytes_accessed=12 << 20, transcendentals=1 << 19),
    )(
        inside(keys),
        inside(own),
        *shifted,
        outside(early),
        outside(late),
        inside(token_kv),
        outside(w_token_qkv),
        outside(w_token_out),
        outside(w_back),
        outside(pooled),
    )
    given = lax.ppermute(give, "col", core_pairs)
    *sent, mixed, joint = pl.pallas_call(
        fold_kernel,
        in_specs=[VMEM] * 3,
        out_specs=[VMEM] * 5,
        out_shape=[folded, folded, folded, pltpu.VMEM((16, 768), F32), stat],
        scratch_shapes=[pltpu.VMEM((2, 128, 128), F32), pltpu.VMEM((4, 16, 768), F32)],
        compiler_params=params(6),
        name="fold",
        cost_estimate=pl.CostEstimate(flops=1 << 26, bytes_accessed=2 << 20, transcendentals=1 << 17),
    )(inside(keep), inside(stats), given)
    parts = [
        lax.ppermute(part, "col", chip_shift(s)) for s, part in zip(FOLD_SHIFTS, sent)
    ]

    scale, diag, low, near, far = pl.pallas_call(
        merge_kernel,
        in_specs=[VMEM] * 9,
        out_specs=[VMEM] * 5,
        out_shape=[
            stat,
            stat,
            pltpu.VMEM((2, 16, 128), BF16),
            jax.ShapeDtypeStruct((16, 128), BF16),
            jax.ShapeDtypeStruct((16, 128), BF16),
        ],
        scratch_shapes=[pltpu.VMEM((4, 128, 128), F32)],
        compiler_params=params(6),
        name="merge",
        cost_estimate=pl.CostEstimate(flops=1 << 26, bytes_accessed=2 << 20, transcendentals=1 << 17),
    )(
        inside(stats),
        inside(mixed),
        inside(joint),
        *parts,
        inside(pooled),
        inside(token_out),
        inside(back),
    )
    near = lax.ppermute(near, "col", core_pairs)
    far = lax.ppermute(far, ("row", "col"), chip_pairs)

    pair_grad = pl.pallas_call(
        pair_grad_kernel,
        in_specs=[VMEM] * 5,
        out_specs=HBM,
        out_shape=jax.ShapeDtypeStruct((128, 256, 128), BF16),
        scratch_shapes=[pltpu.VMEM((128, 256, 128), BF16), pltpu.SemaphoreType.DMA((16,))],
        compiler_params=params(14),
        name="pair_grad",
        cost_estimate=pl.CostEstimate(
            flops=2 * 128 * 256 * 128 * 16 * 8, bytes_accessed=14 << 20, transcendentals=0
        ),
    )(inside(prob), inside(grad), inside(scale), inside(diag), head_rows)
    atom_out = pl.pallas_call(
        atom_out_kernel,
        in_specs=[VMEM] * 4,
        out_specs=VMEM,
        out_shape=jax.ShapeDtypeStruct((128, 128), BF16),
        compiler_params=params(4),
        name="atom_out",
        cost_estimate=pl.CostEstimate(flops=1 << 21, bytes_accessed=1 << 17, transcendentals=0),
    )(far, near, inside(low), inside(hidden))
    return (atom_out, pair_grad.reshape(pair.shape))


def solution(mesh):
    return jax.shard_map(
        shards,
        mesh=mesh,
        in_specs=(
            P(("row", "col"), None),
            P(None, ("row", "col"), None),
            P(("row", "col")),
            P(("row", "col")),
            P(("row", "col")),
            P(("row", "col")),
            P("row", None, "col", None, None),
            P(),
            P(),
            P(),
            P(),
            P(),
            P(),
            P(),
            P(("row", "col"), None),
        ),
        out_specs=(P(("row", "col"), None), P("row", None, "col", None, None)),
        check_vma=False,
    )
```

```python
import functools
import math

import jax
import jax.numpy as jnp
from jax import lax
from jax.experimental import pallas as pl
from jax.experimental.pallas import tpu as pltpu
from jax.sharding import PartitionSpec as P

HA = 4
HT = 16
QB = 32
KW = 128
SHIFT = 16
HALF = 64
GATHER_SHIFTS = (1, 3, 2)
FOLD_SHIFTS = (2, 1, 3)
EARLY = 8
GROUP = 8
AUX = 16
EPSILON = 1e-05
LOWEST = -1e30
MASKED = 1024.0
F32 = jnp.float32
BF16 = jnp.bfloat16
NT = (((1,), (1,)), ((), ()))
TN = (((0,), (0,)), ((), ()))

VMEM = pl.BlockSpec(memory_space=pltpu.VMEM)
HBM = pl.BlockSpec(memory_space=pltpu.HBM)
SMEM = pl.BlockSpec(memory_space=pltpu.SMEM)


def params(mib):
    return pltpu.CompilerParams(vmem_limit_bytes=mib << 20)


def outside(value):
    return pltpu.with_memory_space_constraint(value, pltpu.HBM)


def inside(value):
    return pltpu.with_memory_space_constraint(value, pltpu.VMEM)


def place():
    return lax.axis_index("row"), lax.axis_index("col")


def iota(shape, dim):
    return lax.broadcasted_iota(jnp.int32, shape, dim)


def dot(a, b, dims=None):
    if dims is None:
        return jnp.dot(a, b, preferred_element_type=F32)
    return lax.dot_general(a, b, dims, preferred_element_type=F32)


def normal(values):
    centred = values - jnp.mean(values, axis=-1, keepdims=True)
    return centred * lax.rsqrt(jnp.mean(centred * centred, axis=-1, keepdims=True) + EPSILON)


def split(values):
    high = values.astype(BF16)
    return high, (values - high.astype(F32)).astype(BF16)


def grouped_weight(head_rows, member):
    rows = iota(head_rows.shape, 0)
    return jnp.where(rows % GROUP == member, head_rows, 0.0).astype(BF16)


def pair_bias_kernel(first, pair_ref, head_ref, *refs):
    *brought, tile_ref, bias_ref, arrived, left, came = refs
    extra = len(brought) // 2
    out_ref = brought[extra]
    extras = [
        pltpu.make_async_copy(brought[n], brought[extra + 1 + n], came.at[n]) for n in range(extra)
    ]
    groups = out_ref.shape[0]
    window = min(8, groups)

    def copy(g):
        rows = pl.ds(g * GROUP, GROUP)
        here = pl.ds((g + first) * GROUP, GROUP)
        return pltpu.make_async_copy(pair_ref.at[here], tile_ref.at[rows], arrived.at[g])

    def leave(g):
        return pltpu.make_async_copy(bias_ref.at[g], out_ref.at[g], left.at[g])

    for g in range(window):
        copy(g).start()
    for extra_copy in extras:
        extra_copy.start()
    weight = head_ref[...].astype(F32).reshape(HT, GROUP, 128)[:, 0].astype(BF16)

    def step(g, carry):
        copy(g).wait()
        if window < groups:

            @pl.when(g + window < groups)
            def _():
                copy(g + window).start()

        for i in range(GROUP):
            bias_ref[g, :, i, :] = dot(weight, tile_ref[g * GROUP + i], NT)
        leave(g).start()
        return carry

    lax.fori_loop(0, groups, step, 0, unroll=groups)
    for g in range(groups):
        leave(g).wait()
    for extra_copy in extras:
        extra_copy.wait()


def pack_kernel(
    shift_ref,
    count_ref,
    mask_ref,
    atoms_ref,
    bias_ref,
    cot_ref,
    token_ref,
    near_ref,
    far_ref,
    side_ref,
):
    row, col = place()
    odd = lax.rem(col, 2)
    line = iota((AUX, 128), 0)
    device = row * lax.axis_size("col") + col
    aux = jnp.where(line == 0, token_ref[...] - (16 * device - 17), 0)
    for n in range(4):
        aux = jnp.where(line == 1 + n, shift_ref[n], aux)
    wide = aux.astype(F32)
    aux = wide.astype(BF16)

    def fill(out_ref, at):
        out_ref[0:128] = atoms_ref[...]
        for h in range(HA):
            out_ref[128 + HALF * h : 128 + HALF * (h + 1)] = bias_ref[h, at : at + HALF]
        out_ref[384:448] = cot_ref[at : at + HALF]
        out_ref[448:464] = aux

    side_ref[0:16] = wide
    count = jnp.zeros((16, 128), jnp.int32)
    live = jnp.zeros((16, 128), jnp.int32)
    for t in range(16):
        count = jnp.where(line == t, count_ref[t], count)
        live = jnp.where(line == t, mask_ref[t], live)
    side_ref[16:32] = count.astype(F32)
    side_ref[32:48] = live.astype(F32)

    @pl.when(odd == 1)
    def _():
        fill(near_ref, 0)
        fill(far_ref, HALF)

    @pl.when(odd == 0)
    def _():
        fill(near_ref, HALF)
        fill(far_ref, 0)


def atom_kernel(
    side_ref,
    far_ref,
    near_ref,
    atoms_ref,
    bias_ref,
    cot_ref,
    w_qkv_ref,
    w_out_ref,
    w_pool_ref,
    token_qkv_ref,
    hidden_ref,
    pooled_ref,
    to_row_ref,
    to_col_ref,
    token_kv_ref,
    prev_ref,
    next_ref,
    arrived,
):
    copies = []
    for n in range(4):
        rows = slice(192 * n, 192 * (n + 1))
        copies.append(
            pltpu.make_async_copy(
                token_qkv_ref.at[rows, 768:2304], token_kv_ref.at[rows], arrived.at[n]
            )
        )
    for copy in copies:
        copy.start()
    row, col = place()
    odd = lax.rem(col, 2)
    device = row * lax.axis_size("col") + col
    atom_count = 128 * lax.axis_size("row") * lax.axis_size("col")

    @pl.when(odd == 1)
    def _():
        prev_ref[...] = near_ref[...]
        next_ref[...] = far_ref[...]

    @pl.when(odd == 0)
    def _():
        prev_ref[...] = far_ref[...]
        next_ref[...] = near_ref[...]

    first = device * 128
    extended = jnp.concatenate([prev_ref[0:128], atoms_ref[...], next_ref[0:128]], axis=0)
    wide = extended.astype(F32)
    project = dot(normal(wide).astype(BF16), w_qkv_ref[...]).astype(BF16)
    head_lane = iota((QB, 128), 1) // 32
    head_mask = [jnp.where(head_lane == h, 1.0, 0.0) for h in range(HA)]
    slot = iota((1, KW), 1)
    offset = iota((KW, 160), 1) - iota((KW, 160), 0) - SHIFT
    order = (2, 3, 4, 5, 6, 7, 0, 1)
    biases, shifts, windows, stacks = [], [], [], []
    for block in order:
        if block < 2:
            source, local = prev_ref, block
            shift = prev_ref[451 + local : 452 + local].astype(F32).astype(jnp.int32)
        elif block > 5:
            source, local = next_ref, block - 6
            shift = next_ref[449 + local : 450 + local].astype(F32).astype(jnp.int32)
        else:
            source, local = None, block - 2
            shift = side_ref[1 + local : 2 + local].astype(jnp.int32)
        for h in range(HA):
            if source is None:
                biases.append(bias_ref[h, 32 * local : 32 * local + 32])
            else:
                at = 128 + HALF * h + 32 * local
                biases.append(source[at : at + 32])
        shifts.append(shift)
    for block, shift in zip(order, shifts):
        pick = jnp.where(offset == shift[:, 0:1], 1.0, 0.0).astype(BF16)
        windows.append(dot(pick, project[32 * block : 32 * block + 160, 128:]).astype(BF16))
        query = project[64 + 32 * block : 96 + 32 * block, :128].astype(F32)
        stacks.append(
            jnp.concatenate([query * head_mask[h] for h in range(HA)], axis=0).astype(BF16)
        )
    scores = [
        dot(stack, window[:, :128], NT) * (1.0 / math.sqrt(32))
        for stack, window in zip(stacks, windows)
    ]
    weights = []
    for n, block in enumerate(order):
        score = scores[n] + jnp.concatenate(biases[HA * n : HA * n + HA], axis=0).astype(F32)
        position = slot + (first + 32 * block - 112) + shifts[n]
        inside = (position >= 0) & (position < atom_count)
        score = jnp.where(inside, score, LOWEST)
        raised = jnp.exp(score - jnp.max(score, axis=-1, keepdims=True))
        weights.append((raised / jnp.sum(raised, axis=-1, keepdims=True)).astype(BF16))
    mixes = []
    for weight, window in zip(weights, windows):
        mixed = dot(weight, window[:, 128:])
        mix = mixed[0:32] * head_mask[0]
        for h in range(1, HA):
            mix = mix + mixed[32 * h : 32 * h + 32] * head_mask[h]
        mixes.append(mix)
    mixture = jnp.concatenate(mixes, axis=0).astype(BF16)
    base = jnp.concatenate([wide[128:320], wide[64:128]], axis=0)
    hidden = (base + dot(mixture, w_out_ref[...])).astype(BF16)
    hidden_ref[0:128] = hidden[:128]
    relative = side_ref[0:1] - 1.0
    hidden_ref[128:144] = jnp.broadcast_to(relative, (16, 128)).astype(BF16)
    lifted = jnp.maximum(dot(hidden, w_pool_ref[...]), 0.0)
    own_token = side_ref[0:1] - 17.0
    prev_token = prev_ref[448:449].astype(F32) - 33.0
    next_token = next_ref[448:449].astype(F32) - 1.0
    beside = jnp.where(iota((1, 128), 1) < HALF, next_token, prev_token)
    token = jnp.concatenate([own_token, beside], axis=1)
    select = jnp.where(iota((16, 256), 0).astype(F32) == token, 1.0, 0.0).astype(BF16)
    high, low = split(lifted)
    count = jnp.concatenate([side_ref[16:32]] * 6, axis=1)
    pooled = (dot(select, high) + dot(select, low)) / count
    pooled_ref[...] = pooled
    normed = normal(pooled).astype(BF16)
    cot = jnp.concatenate([cot_ref[...], next_ref[384:448], prev_ref[384:448]], axis=0)
    grad_up = dot(select, cot).astype(BF16)
    live = jnp.concatenate([side_ref[32:48]] * 6, axis=1)
    marked = jnp.where(live > 0, normed.astype(F32), MASKED).astype(BF16)
    for r in range(to_row_ref.shape[0]):
        to_row_ref[r] = marked
    to_col_ref[:, :768] = normed
    to_col_ref[:, 768:] = grad_up
    for copy in copies:
        copy.wait()


def window_of(head):
    block, rest = divmod(head, 8)
    return 384 * block + (0 if rest < 5 else 128)


def stack_kernel(own_ref, partner_ref, out_ref):
    row, col = place()
    core = lax.rem(col, 2)
    out_ref[core] = own_ref[...]
    out_ref[1 - core] = partner_ref[...]


def token_kernel(
    keys_ref,
    own_ref,
    first_ref,
    second_ref,
    third_ref,
    early_ref,
    late_ref,
    w_kv_ref,
    w_qkv_ref,
    w_out_ref,
    w_back_ref,
    pooled_ref,
    prob_ref,
    grad_ref,
    stats_ref,
    keep_ref,
    give_ref,
    pooled_out_ref,
    inner_out_ref,
    inner_back_ref,
    rows_ref,
    mixed_ref,
    inner_ref,
    bias_ref,
    arrived,
):
    copies = []
    for n in range(2):
        rows = slice(384 * n, 384 * (n + 1))
        copies.append((w_qkv_ref.at[rows, 0:768], inner_ref.at[rows]))
    copies.append((w_back_ref, inner_back_ref))
    for n in range(2):
        rows = slice(384 * n, 384 * (n + 1))
        copies.append((w_out_ref.at[rows], inner_out_ref.at[rows]))
    early = early_ref.shape[0]
    for first, count, source in ((0, early, early_ref), (early, 16 - early, late_ref)):
        for start, stop in ((0, count // 2), (count // 2, count)):
            copies.append(
                (source.at[start:stop], bias_ref.at[first + start : first + stop])
            )
    copies.append((pooled_ref, pooled_out_ref))
    copies = [pltpu.make_async_copy(a, b, arrived.at[n]) for n, (a, b) in enumerate(copies)]
    for copy in copies[:5]:
        copy.start()

    row, col = place()
    chip, core = lax.div(col, 2), lax.rem(col, 2)
    parts = (own_ref, first_ref, second_ref, third_ref)
    for s, part_ref in zip((0,) + GATHER_SHIFTS, parts):
        there = lax.rem(chip + 4 - s, 4) * 32
        rows_ref[pl.ds(pl.multiple_of(there, 32), 16)] = part_ref[0]
        rows_ref[pl.ds(pl.multiple_of(there + 16, 16), 16)] = part_ref[1]
    key = dot(keys_ref[...], w_kv_ref[:, :768]).astype(BF16)
    value = dot(keys_ref[...], w_kv_ref[:, 768:]).astype(BF16)
    for copy in copies[5:]:
        copy.start()
    for copy in copies[:2]:
        copy.wait()
    query = dot(rows_ref[:, :768], inner_ref[...]).astype(BF16)
    for copy in copies[2:5]:
        copy.wait()
    middle = dot(rows_ref[:, 768:], inner_back_ref[...], NT).astype(BF16)
    grad = dot(middle, inner_out_ref[...], NT).astype(BF16)
    first = keys_ref[:, :128].astype(F32).T[0:1]
    closed = jnp.where(first < MASKED, 0.0, -jnp.inf)
    lane = iota((128, 256), 1)
    stat_lane = iota((128, 128), 1)

    def within(h):
        at = window_of(h)
        return (lane >= 48 * h - at) & (lane < 48 * (h + 1) - at)

    for h in range(HT):
        at = window_of(h)
        grad_h = jnp.where(within(h), grad[:, at : at + 256].astype(F32), 0.0).astype(BF16)
        grads = dot(grad_h, value[:, at : at + 256], NT)
        grad_ref[:, h] = grads.reshape(16, GROUP, 256)
    for copy in copies[5:]:
        copy.wait()
    for h in range(HT):
        at = window_of(h)
        query_h = jnp.where(within(h), query[:, at : at + 256].astype(F32), 0.0).astype(BF16)
        scores = dot(query_h, key[:, at : at + 256], NT) * (1.0 / math.sqrt(48))
        bias = bias_ref[:, h].reshape(128, 256)
        prob_ref[:, h] = (scores + bias + closed).reshape(16, GROUP, 256)
    tops = jnp.zeros((128, 128), F32)
    sums = jnp.zeros((128, 128), F32)
    diags = jnp.zeros((128, 128), F32)
    for h in range(HT):
        scores = prob_ref[:, h].reshape(128, 256)
        top = jnp.maximum(jnp.max(scores, axis=-1, keepdims=True), LOWEST)
        high = top.astype(BF16).astype(F32)
        top = high + (top - high).astype(BF16).astype(F32)
        raised = jnp.exp(scores - top)
        prob_ref[:, h] = raised.reshape(16, GROUP, 256)
        total = jnp.sum(raised, axis=-1, keepdims=True)
        diag = jnp.sum(raised * grad_ref[:, h].reshape(128, 256), axis=-1, keepdims=True)
        here = stat_lane == h
        tops = jnp.where(here, top, tops)
        sums = jnp.where(here, total, sums)
        diags = jnp.where(here, diag, diags)
    for at in (0, 128, 384, 512):
        out = None
        for h in range(HT):
            if window_of(h) == at:
                raised = prob_ref[:, h].reshape(128, 256).astype(BF16)
                part = jnp.where(within(h), dot(raised, value[:, at : at + 256]), 0.0)
                out = part if out is None else out + part
        if at % 384 == 0:
            mixed_ref[:, at : at + 256] = out
        else:
            mixed_ref[:, at : at + 128] = mixed_ref[:, at : at + 128] + out[:, :128]
            mixed_ref[:, at + 128 : at + 256] = out[:, 128:]
    stats_ref[...] = tops + pltpu.roll(sums, 32, axis=1) + pltpu.roll(diags, 64, axis=1)
    packed = packed_stats(tops, sums, diags)
    for n in range(4):
        there = 32 * n + 16 * core
        keep_ref[n] = mixed_ref[pl.ds(pl.multiple_of(there, 16), 16)]
        there = 32 * n + 16 - 16 * core
        part = mixed_ref[pl.ds(pl.multiple_of(there, 16), 16)]
        give_ref[n, :, :768] = part.astype(BF16)
        for k in range(2):
            at = 32 * n + 16 * k
            give_ref[n, :, 768 + 128 * k : 896 + 128 * k] = packed[at : at + 16]


def packed_stats(tops, sums, diags):
    stats = jnp.zeros((128, 128), F32)
    for k, part in enumerate((tops, sums, diags)):
        high = part.astype(BF16).astype(F32)
        for n, piece in enumerate((high, part - high)):
            turn = 32 * k + 16 * n
            stats = stats + (pltpu.roll(piece, turn, axis=1) if turn else piece)
    return stats.astype(BF16)


def spread_heads(factors):
    spread = jnp.where(iota((128, 768), 1) // 48 == iota((128, 768), 0), 1.0, 0.0).astype(BF16)
    high, low = split(factors)
    return dot(high, spread) + dot(low, spread)


def parted_stats(stats):
    lane = iota((128, 128), 1)
    parts = [stats, pltpu.roll(stats, 96, axis=1), pltpu.roll(stats, 64, axis=1)]
    return [jnp.where(lane < HT, part, 0.0) for part in parts]


def fold_kernel(
    keep_ref,
    stats_ref,
    given_ref,
    first_ref,
    second_ref,
    third_ref,
    own_ref,
    joint_ref,
    ratio_ref,
    mixed_ref,
):
    row, col = place()
    chip, core = lax.div(col, 2), lax.rem(col, 2)
    given = jnp.concatenate(
        [given_ref[n, :, 768 + 128 * k : 896 + 128 * k] for n in range(4) for k in range(2)],
        axis=0,
    ).astype(F32)
    given = given + pltpu.roll(given, 112, axis=1)
    sides = [parted_stats(stats_ref[...]), parted_stats(given)]
    top = jnp.maximum(sides[0][0], sides[1][0])
    ratios = [jnp.exp(side[0] - top) for side in sides]
    total = ratios[0] * sides[0][1] + ratios[1] * sides[1][1]
    diag = ratios[0] * sides[0][2] + ratios[1] * sides[1][2]
    joint_ref[...] = top + pltpu.roll(total, 32, axis=1) + pltpu.roll(diag, 64, axis=1)
    ratio_ref[0] = ratios[0]
    ratio_ref[1] = ratios[1]
    rows = [pl.ds(pl.multiple_of(32 * n + 16 * core, 16), 16) for n in range(4)]
    factors = spread_heads(
        jnp.concatenate([ratio_ref[side, rows[n]] for side in range(2) for n in range(4)], axis=0)
    )
    for n in range(4):
        given_n = given_ref[n, :, :768].astype(F32)
        mixed_ref[n] = (
            keep_ref[n] * factors[16 * n : 16 * n + 16]
            + given_n * factors[64 + 16 * n : 80 + 16 * n]
        )
    packed = packed_stats(top, total, diag)
    for s, out_ref in zip(FOLD_SHIFTS, (first_ref, second_ref, third_ref)):
        out_ref[:, :768] = mixed_ref[lax.rem(chip + s, 4)].astype(BF16)
        for k in range(8):
            out_ref[:, 768 + 128 * k : 896 + 128 * k] = packed[16 * k : 16 * k + 16]
    own_ref[...] = mixed_ref[chip]


def merge_kernel(
    stats_ref,
    own_ref,
    joint_ref,
    first_ref,
    second_ref,
    third_ref,
    pooled_ref,
    w_out_ref,
    w_back_ref,
    scale_ref,
    diag_ref,
    low_ref,
    near_ref,
    far_ref,
    ratio_ref,
):
    row, col = place()
    lane = iota((128, 128), 1)
    sides = [parted_stats(joint_ref[...])]
    for part_ref in (first_ref, second_ref, third_ref):
        stats = jnp.concatenate(
            [part_ref[:, 768 + 128 * k : 896 + 128 * k] for k in range(8)], axis=0
        ).astype(F32)
        sides.append(parted_stats(stats + pltpu.roll(stats, 112, axis=1)))
    top = functools.reduce(jnp.maximum, [side[0] for side in sides])
    ratios = [jnp.exp(side[0] - top) for side in sides]
    total = functools.reduce(jnp.add, [r * side[1] for r, side in zip(ratios, sides)])
    diag = functools.reduce(jnp.add, [r * side[2] for r, side in zip(ratios, sides)])
    inverse = 1.0 / jnp.where(lane < HT, total, 1.0)
    for n in range(4):
        ratio_ref[n] = ratios[n] * inverse
    own_top = parted_stats(stats_ref[...])[0]
    scale_ref[...] = jnp.exp(own_top - top) * inverse
    diag_ref[...] = diag * inverse
    rows = pl.ds(pl.multiple_of(col * 16, 16), 16)
    factors = spread_heads(jnp.concatenate([ratio_ref[n, rows] for n in range(4)], axis=0))
    mixed = own_ref[...] * factors[0:16]
    for n, part_ref in enumerate((first_ref, second_ref, third_ref)):
        mixed = mixed + part_ref[:, :768].astype(F32) * factors[16 * n + 16 : 16 * n + 32]
    updated = (pooled_ref[...] + dot(mixed.astype(BF16), w_out_ref[...])).astype(BF16)
    high, low = split(dot(updated, w_back_ref[...]))
    near_ref[...] = high
    far_ref[...] = high
    low_ref[0] = high
    low_ref[1] = low


def pair_grad_kernel(prob_ref, grad_ref, scale_ref, diag_ref, head_ref, out_ref, tile_ref, left):
    groups = prob_ref.shape[0]

    def copy(g):
        rows = pl.ds(g * GROUP, GROUP)
        return pltpu.make_async_copy(tile_ref.at[rows], out_ref.at[rows], left.at[g])

    head_rows = head_ref[...].astype(F32)
    weights = jnp.concatenate([grouped_weight(head_rows, i) for i in range(GROUP)], axis=1)

    def score_of(g):
        rows = pl.ds(pl.multiple_of(g * GROUP, GROUP), GROUP)
        scale = scale_ref[rows]
        diag = diag_ref[rows]
        score = jnp.concatenate(
            [
                prob_ref[g, h] * scale[:, h : h + 1] * (grad_ref[g, h] - diag[:, h : h + 1])
                for h in range(HT)
            ],
            axis=0,
        )
        return score.T.astype(BF16)

    def step(g, score):
        following = score_of(jnp.minimum(g + 1, groups - 1))
        result = dot(score, weights)
        for i in range(GROUP):
            tile_ref[g * GROUP + i] = result[:, 128 * i : 128 * (i + 1)].astype(BF16)
        copy(g).start()
        return following

    lax.fori_loop(0, groups, step, score_of(0), unroll=groups)
    for g in range(groups):
        copy(g).wait()


def atom_out_kernel(far_ref, near_ref, low_ref, hidden_ref, out_ref):
    row, col = place()
    odd = lax.rem(col, 2) == 1
    near = near_ref[...].astype(F32)
    far = far_ref[...].astype(F32)
    before = jnp.where(odd, near, far).astype(BF16)
    after = jnp.where(odd, far, near).astype(BF16)
    rows = jnp.concatenate([before, low_ref[0], after, low_ref[1]], axis=0)
    token = hidden_ref[128:144].astype(F32)[0:1]
    index = iota((64, 128), 0)
    index = jnp.where(index < 48, index, index - 32).astype(F32)
    select = jnp.where(index == token, 1.0, 0.0).astype(BF16)
    out_ref[...] = (hidden_ref[0:128].astype(F32) + dot(select, rows, TN)).astype(BF16)


def shards(
    atoms,
    atom_bias,
    key_shift,
    atom_token,
    token_atoms,
    token_mask,
    pair,
    w_atom_qkv,
    w_atom_out,
    w_pool,
    w_token_qkv,
    w_token_out,
    w_bias,
    w_back,
    cotangent,
):
    row_count, col_count = lax.axis_size("row"), lax.axis_size("col")
    devices = row_count * col_count
    core_pairs = [(i, i ^ 1) for i in range(col_count)]
    chip_pairs = [(i, i + 1) for i in range(1, devices - 1, 2)]
    chip_pairs = chip_pairs + [(j, i) for i, j in chip_pairs]

    def chip_shift(steps):
        return [(i, (i + 2 * steps) % col_count) for i in range(col_count)]

    tokens = atom_token.reshape(1, 128)
    payload = jax.ShapeDtypeStruct((464, 128), BF16)
    near, far, side = pl.pallas_call(
        pack_kernel,
        in_specs=[SMEM] * 3 + [VMEM] * 4,
        out_specs=[VMEM] * 3,
        out_shape=[payload, payload, pltpu.VMEM((48, 128), F32)],
        compiler_params=params(4),
        name="pack",
        cost_estimate=pl.CostEstimate(flops=0, bytes_accessed=1 << 20, transcendentals=0),
    )(
        outside(key_shift),
        outside(token_atoms),
        outside(token_mask),
        outside(atoms),
        outside(atom_bias),
        outside(cotangent),
        outside(tokens),
    )
    near = lax.ppermute(near, "col", core_pairs)
    far = lax.ppermute(far, ("row", "col"), chip_pairs)

    tile = pair.reshape(128, 256, 128)
    head_rows = jnp.repeat(jnp.transpose(w_bias), GROUP, axis=0)
    def pair_bias(first, groups, name, *brought):
        return pl.pallas_call(
            functools.partial(pair_bias_kernel, first),
            in_specs=[HBM, VMEM] + [HBM] * len(brought),
            out_specs=[HBM] + [VMEM] * len(brought),
            out_shape=[pltpu.HBM((groups, HT, GROUP, 256), F32)]
            + [pltpu.VMEM(value.shape, value.dtype) for value in brought],
            scratch_shapes=[
                pltpu.VMEM((groups * GROUP, 256, 128), BF16),
                pltpu.VMEM((groups, HT, GROUP, 256), F32),
                pltpu.SemaphoreType.DMA((groups,)),
                pltpu.SemaphoreType.DMA((groups,)),
                pltpu.SemaphoreType.DMA((max(len(brought), 1),)),
            ],
            compiler_params=params(14),
            name=name,
            cost_estimate=pl.CostEstimate(
                flops=groups << 26, bytes_accessed=groups << 19, transcendentals=0
            ),
        )(outside(tile), head_rows, *[outside(value) for value in brought])

    half = EARLY
    early, *atom_inputs = pair_bias(
        0,
        half,
        "pair_bias_early",
        atoms,
        atom_bias,
        cotangent,
        w_atom_qkv,
        w_atom_out,
        w_pool,
    )
    (late,) = pair_bias(half, 16 - half, "pair_bias_late")

    hidden, pooled, to_row, to_col, token_kv = pl.pallas_call(
        atom_kernel,
        in_specs=[VMEM] * 9 + [HBM],
        out_specs=[VMEM] * 5,
        out_shape=[
            pltpu.VMEM((144, 128), BF16),
            pltpu.HBM((16, 768), F32),
            pltpu.VMEM((row_count, 16, 768), BF16),
            pltpu.VMEM((16, 896), BF16),
            pltpu.VMEM((768, 1536), BF16),
        ],
        scratch_shapes=[
            pltpu.VMEM((464, 128), BF16),
            pltpu.VMEM((464, 128), BF16),
            pltpu.SemaphoreType.DMA((4,)),
        ],
        compiler_params=params(8),
        name="atom_stage",
        cost_estimate=pl.CostEstimate(flops=1 << 28, bytes_accessed=2 << 20, transcendentals=1 << 17),
    )(
        inside(side),
        far,
        near,
        *[inside(value) for value in atom_inputs],
        outside(w_token_qkv),
    )
    partner = lax.ppermute(to_col, "col", core_pairs)
    keys = lax.all_to_all(to_row, "row", 0, 0).reshape(256, 768)
    own = pl.pallas_call(
        stack_kernel,
        in_specs=[VMEM] * 2,
        out_specs=VMEM,
        out_shape=pltpu.VMEM((2, 16, 896), BF16),
        compiler_params=params(4),
        name="stack",
        cost_estimate=pl.CostEstimate(flops=1 << 32, bytes_accessed=1 << 18, transcendentals=0),
    )(inside(to_col), partner)
    shifted = [lax.ppermute(own, "col", chip_shift(s)) for s in GATHER_SHIFTS]

    stat = pltpu.VMEM((128, 128), F32)
    swapped = jax.ShapeDtypeStruct((4, 16, 1024), BF16)
    folded = jax.ShapeDtypeStruct((16, 1792), BF16)
    table = pltpu.VMEM((16, HT, GROUP, 256), F32)
    prob, grad, stats, keep, give, pooled, token_out, back = pl.pallas_call(
        token_kernel,
        in_specs=[VMEM] * 5 + [HBM] * 2 + [VMEM] + [HBM] * 4,
        out_specs=[VMEM] * 8,
        scratch_shapes=[
            pltpu.VMEM((128, 896), BF16),
            pltpu.VMEM((128, 768), F32),
            pltpu.VMEM((768, 768), BF16),
            pltpu.VMEM((16, HT, GROUP, 256), F32),
            pltpu.SemaphoreType.DMA((10,)),
        ],
        out_shape=[
            table,
            table,
            stat,
            pltpu.VMEM((4, 16, 768), F32),
            swapped,
            pltpu.VMEM((16, 768), F32),
            pltpu.VMEM(w_token_out.shape, BF16),
            pltpu.VMEM(w_back.shape, BF16),
        ],
        compiler_params=params(16),
        name="token_stage",
        cost_estimate=pl.CostEstimate(flops=1 << 31, bytes_accessed=12 << 20, transcendentals=1 << 19),
    )(
        inside(keys),
        inside(own),
        *shifted,
        outside(early),
        outside(late),
        inside(token_kv),
        outside(w_token_qkv),
        outside(w_token_out),
        outside(w_back),
        outside(pooled),
    )
    given = lax.ppermute(give, "col", core_pairs)
    *sent, mixed, joint = pl.pallas_call(
        fold_kernel,
        in_specs=[VMEM] * 3,
        out_specs=[VMEM] * 5,
        out_shape=[folded, folded, folded, pltpu.VMEM((16, 768), F32), stat],
        scratch_shapes=[pltpu.VMEM((2, 128, 128), F32), pltpu.VMEM((4, 16, 768), F32)],
        compiler_params=params(6),
        name="fold",
        cost_estimate=pl.CostEstimate(flops=1 << 26, bytes_accessed=2 << 20, transcendentals=1 << 17),
    )(inside(keep), inside(stats), given)
    parts = [
        lax.ppermute(part, "col", chip_shift(s)) for s, part in zip(FOLD_SHIFTS, sent)
    ]

    scale, diag, low, near, far = pl.pallas_call(
        merge_kernel,
        in_specs=[VMEM] * 9,
        out_specs=[VMEM] * 5,
        out_shape=[
            stat,
            stat,
            pltpu.VMEM((2, 16, 128), BF16),
            jax.ShapeDtypeStruct((16, 128), BF16),
            jax.ShapeDtypeStruct((16, 128), BF16),
        ],
        scratch_shapes=[pltpu.VMEM((4, 128, 128), F32)],
        compiler_params=params(6),
        name="merge",
        cost_estimate=pl.CostEstimate(flops=1 << 26, bytes_accessed=2 << 20, transcendentals=1 << 17),
    )(
        inside(stats),
        inside(mixed),
        inside(joint),
        *parts,
        inside(pooled),
        inside(token_out),
        inside(back),
    )
    near = lax.ppermute(near, "col", core_pairs)
    far = lax.ppermute(far, ("row", "col"), chip_pairs)

    pair_grad = pl.pallas_call(
        pair_grad_kernel,
        in_specs=[VMEM] * 5,
        out_specs=HBM,
        out_shape=jax.ShapeDtypeStruct((128, 256, 128), BF16),
        scratch_shapes=[pltpu.VMEM((128, 256, 128), BF16), pltpu.SemaphoreType.DMA((16,))],
        compiler_params=params(14),
        name="pair_grad",
        cost_estimate=pl.CostEstimate(
            flops=2 * 128 * 256 * 128 * 16 * 8, bytes_accessed=14 << 20, transcendentals=0
        ),
    )(inside(prob), inside(grad), inside(scale), inside(diag), head_rows)
    atom_out = pl.pallas_call(
        atom_out_kernel,
        in_specs=[VMEM] * 4,
        out_specs=VMEM,
        out_shape=jax.ShapeDtypeStruct((128, 128), BF16),
        compiler_params=params(4),
        name="atom_out",
        cost_estimate=pl.CostEstimate(flops=1 << 21, bytes_accessed=1 << 17, transcendentals=0),
    )(far, near, inside(low), inside(hidden))
    return (atom_out, pair_grad.reshape(pair.shape))


def solution(mesh):
    return jax.shard_map(
        shards,
        mesh=mesh,
        in_specs=(
            P(("row", "col"), None),
            P(None, ("row", "col"), None),
            P(("row", "col")),
            P(("row", "col")),
            P(("row", "col")),
            P(("row", "col")),
            P("row", None, "col", None, None),
            P(),
            P(),
            P(),
            P(),
            P(),
            P(),
            P(),
            P(("row", "col"), None),
        ),
        out_specs=(P(("row", "col"), None), P("row", None, "col", None, None)),
        check_vma=False,
    )
```
